32 devices in a mesh: row: 4 (over x, core), col: 8 (over z, y).
Axes of the slice: x: 2, y: 2, z: 4, core: 2. Of those that a mesh axis runs over, the one named last changes fastest.
Arguments:
- inputs: bfloat16 [512, 6144], P(('row', 'col')), may hold values from -6 to 6
- cotangent: bfloat16 [512, 6144], P(('row', 'col')), may hold values from -0.41992188 to 0.41992188
- w_in: bfloat16 [1536, 24576], P('row', 'col'), may hold values from -0.15625 to 0.15625
- w_out: bfloat16 [1536, 24576], P('row', 'col'), may hold values from -0.078125 to 0.078125
- keep_in: int32 [192, 12], replicated, may hold values from 0 to 47, all different within a row
- keep_out: int32 [192, 12], replicated, may hold values from 0 to 47, all different within a row
Outputs:
- grad_in: bfloat16 [1536, 24576], P('row', 'col')
- grad_out: bfloat16 [1536, 24576], P('row', 'col')
The draws below stay inside these ranges and needn't reach their ends.
Inputs may be any that keep to these rules, and one draw needn't show every extreme that they name: `keep_in`: each row names 12 different input blocks, and every block is named by some row. `keep_out`: each row names 12 different output blocks, and every block is named by some row.
All inputs are finite; a program needn't handle non-finite values.
Results may differ from the reference program's by a relative error of at most 0.022.
Values may be sent and summed in bfloat16 or wider, within the bound.
No kernel may reach another device: no remote copies, remote signals or barrier semaphores. Data moves between devices by JAX's collectives and lax.ppermute only.
A program may use at most 128 MiB of HBM per device.

```python
import jax
import jax.numpy as jnp
from jax import lax

D = 6144
FF = 24576
BLK = 128
TOK = 128
KEEP = 12
TOKENS = 512
NBF = 192


def steps_of(rng, shape, split, smallest, top_value):
    gain = 1.0
    for axis_at, blocks in split:
        draws = jax.random.uniform(jax.random.fold_in(jax.random.fold_in(rng, 6), axis_at), (blocks,), jnp.float32, smallest / len(split), top_value / len(split))
        gain = gain * jnp.repeat(jnp.exp(draws), shape[axis_at] // blocks).reshape((-1,) + (1,) * (len(shape) - 1 - axis_at))
    return gain


def choose_distinct(stream_key, rows, count, top, lift):
    ranking = jax.random.permutation(jax.random.fold_in(stream_key, 1), count)
    favour = ranking
    for power in range(3):
        favour = favour * favour // count
    favour = favour * lift // count
    lots = jax.random.randint(jax.random.fold_in(stream_key, 2), (rows, count), 0, 4096) + favour
    holders = jax.random.permutation(jax.random.fold_in(stream_key, 3), rows)[jnp.arange(count) % rows]
    lots = jnp.where(jnp.arange(rows)[:, None] == holders[None, :], 1 << 14, lots)
    priority = lots * count + jnp.arange(count)
    return lax.top_k(priority.astype(jnp.int32), top)[1].astype(jnp.int32)


def bell_draw(rng, dims, scale, limit, cuts=(), kind=jnp.bfloat16):
    entries = scale * jax.random.normal(rng, dims, jnp.float32)
    if cuts:
        entries = entries * steps_of(rng, dims, cuts, -0.22, 0.18)
    return jnp.clip(entries, -limit, limit).astype(kind)


def setup_inputs(seed: int = 0) -> dict:
    keys = jax.random.split(jax.random.key(seed), 7)
    inputs = bell_draw(keys[0], (TOKENS, D), 1.0, 6.0, ((0, 32),))
    cotangent = bell_draw(keys[1], (TOKENS, D), 0.07, 0.41992188, ((0, 32),))
    w_in = bell_draw(keys[2], (KEEP * BLK, FF), (D // 4) ** -0.5, 0.15625, ((0, 4), (1, 8)))
    w_out = bell_draw(keys[3], (KEEP * BLK, FF), (FF // 4) ** -0.5, 0.078125, ((0, 4), (1, 8)))
    keep_in = choose_distinct(keys[4], NBF, D // BLK, KEEP, 0)
    keep_out = choose_distinct(keys[5], NBF, D // BLK, KEEP, 0)
    return {"inputs": inputs, "cotangent": cotangent, "w_in": w_in, "w_out": w_out, "keep_in": keep_in, "keep_out": keep_out}


def gelu_tanh(values):
    return jax.nn.gelu(values, approximate=True)

def select_blocks(matrix, chosen):
    rows = matrix.shape[0]
    blocks = matrix.reshape(rows, D // BLK, BLK)
    return jnp.take(blocks, chosen, axis=1).reshape(rows, KEEP * BLK)

def group_sum(left, right):
    groups = TOKENS // TOK
    terms = jnp.einsum('gts,gtq->gsq', left.reshape(groups, TOK, KEEP * BLK).astype(jnp.float32), right.reshape(groups, TOK, BLK).astype(jnp.float32))
    rounded = lax.optimization_barrier(terms.astype(jnp.bfloat16))
    return lax.optimization_barrier(jnp.sum(rounded.astype(jnp.float32), axis=0)).astype(jnp.bfloat16)

def reference(inputs, cotangent, w_in, w_out, keep_in, keep_out):

    def one_block(index):
        picked_in = select_blocks(inputs, keep_in[index])
        picked_out = select_blocks(cotangent, keep_out[index])
        panel_in = lax.dynamic_slice_in_dim(w_in, index * BLK, BLK, 1)
        panel_out = lax.dynamic_slice_in_dim(w_out, index * BLK, BLK, 1)
        hidden = jnp.dot(picked_in, panel_in, preferred_element_type=jnp.float32)
        d_act = jnp.dot(picked_out, panel_out, preferred_element_type=jnp.float32)
        act, pullback = jax.vjp(gelu_tanh, hidden)
        d_hidden = pullback(d_act)[0].astype(jnp.bfloat16)
        act = act.astype(jnp.bfloat16)
        return (group_sum(picked_in, d_hidden), group_sum(picked_out, act))
    grad_in, grad_out = lax.map(one_block, jnp.arange(FF // BLK, dtype=jnp.int32))
    grad_in = jnp.transpose(grad_in, (1, 0, 2)).reshape(KEEP * BLK, FF)
    grad_out = jnp.transpose(grad_out, (1, 0, 2)).reshape(KEEP * BLK, FF)
    return (grad_in, grad_out)
```

```python
import functools

import jax
import jax.numpy as jnp
from jax import lax
from jax.experimental import pallas as pl
from jax.experimental.pallas import tpu as pltpu
from jax.sharding import PartitionSpec as P

D = 6144
BLK = 128
KEEP = 12
ROWS = 4
COLS = 8
LANES = 4
SCALE = 0.7978845608028654
CUBIC = 0.044715
VMEM_LIMIT = 56 * 1024 * 1024


def gelu_tanh(values):
    return jax.nn.gelu(values, approximate=True)


def pick_one(matrix, chosen):
    return jnp.take(matrix, chosen, axis=1)


def general(inputs, cotangent, w_in, w_out, keep_in, keep_out):
    width = w_in.shape[1]
    blocks_here = width // BLK
    kept_rows = w_in.shape[0]
    column = lax.axis_index("col")
    own_in = lax.dynamic_slice_in_dim(keep_in, column * blocks_here, blocks_here, 0)
    own_out = lax.dynamic_slice_in_dim(keep_out, column * blocks_here, blocks_here, 0)
    tables = jnp.stack((own_in, own_out), 0)
    stacked = jnp.stack((inputs, cotangent), 0)
    whole = lax.all_gather(stacked, "col", axis=1, tiled=True)
    tokens_here = whole.shape[1]
    blocks = whole.reshape(2, tokens_here, D // BLK, BLK)
    picked = jax.vmap(pick_one)(blocks, tables).reshape(2, tokens_here, blocks_here, KEEP * BLK)
    weights = jnp.stack((w_in, w_out), 1)
    full = lax.all_gather(weights, "row", axis=0, tiled=True)
    panel = full.reshape(KEEP * BLK, 2, blocks_here, BLK)
    mixed = jnp.einsum("ptck,kpcq->ptcq", picked, panel, preferred_element_type=jnp.float32)
    hidden = mixed[0].reshape(tokens_here, width)
    d_act = mixed[1].reshape(tokens_here, width)
    act, pullback = jax.vjp(gelu_tanh, hidden)
    d_hidden = pullback(d_act)[0].astype(jnp.bfloat16)
    act = act.astype(jnp.bfloat16)
    paired = jnp.stack((d_hidden, act), 0).reshape(2, tokens_here, blocks_here, BLK)
    term = jnp.einsum("ptck,ptcq->kpcq", picked, paired, preferred_element_type=jnp.float32)
    summed = (
        lax.psum_scatter(
            term.reshape(lax.axis_size("row") * kept_rows, 2 * width).astype(jnp.bfloat16),
            "row",
            scatter_dimension=0,
            tiled=True,
        )
        .astype(jnp.float32)
        .reshape(kept_rows, 2, width)
    )
    return (summed[:, 0].astype(jnp.bfloat16), summed[:, 1].astype(jnp.bfloat16))


def picked_rows(table, buffers, side, block, slots):
    columns = []
    for slot in range(slots):
        start = pl.multiple_of(table[(block * 2 + side) * slots + slot] * BLK, BLK)
        columns.append(jnp.concatenate([buf[side, :, pl.ds(start, BLK)] for buf in buffers], axis=0))
    return jnp.concatenate(columns, axis=1)


def partial_kernel(n_buf, slots, table, *refs):
    buffers = refs[:n_buf]
    own = refs[n_buf : n_buf + 2]
    sib = refs[n_buf + 2 : n_buf + 4]
    keep_ref, send_ref = refs[n_buf + 4 :]
    step = pl.program_id(0)
    for lane in range(LANES):
        at = slice(lane * BLK, (lane + 1) * BLK)
        for side in range(2):
            left = picked_rows(table, buffers, side, step * LANES + lane, slots)
            right = jnp.concatenate((own[side][:, at], sib[side][:, at]), axis=0)
            total = jnp.dot(left, right, preferred_element_type=jnp.float32)
            keep_ref[side, :, at] = total
            send_ref[side, :, at] = total.astype(jnp.bfloat16)


def partial(table, buffers, w_in, w_out, s_in, s_out, core):
    tokens = sum(b.shape[1] for b in buffers)
    half = s_in.shape[1]
    kept = w_in.shape[0]
    wide = LANES * BLK
    steps = half // wide
    slots = 2 * kept // BLK
    core_at = table.shape[0] - 1
    whole = [pl.BlockSpec(b.shape, lambda g, t: (0, 0, 0)) for b in buffers]
    own = pl.BlockSpec((kept, wide), lambda g, t: (0, t[core_at] * steps + g))
    sib = pl.BlockSpec((kept, wide), lambda g, t: (0, g))
    out = pl.BlockSpec((2, tokens, wide), lambda g, t: (0, 0, g))
    return pl.pallas_call(
        functools.partial(partial_kernel, len(buffers), slots),
        grid_spec=pltpu.PrefetchScalarGridSpec(
            num_scalar_prefetch=1,
            grid=(steps,),
            in_specs=whole + [own, own, sib, sib],
            out_specs=[out, out],
        ),
        out_shape=[
            jax.ShapeDtypeStruct((2, tokens, half), jnp.float32),
            jax.ShapeDtypeStruct((2, tokens, half), jnp.bfloat16),
        ],
        compiler_params=pltpu.CompilerParams(vmem_limit_bytes=VMEM_LIMIT),
        cost_estimate=pl.CostEstimate(flops=1000, bytes_accessed=1000, transcendentals=0),
        name="partial",
    )(table, *buffers, w_in, w_out, s_in, s_out)


def grad_kernel(n_buf, slots, first, last, table, *refs):
    buffers = refs[:n_buf]
    keep_ref, got_ref = refs[n_buf : n_buf + 2]
    refs = refs[n_buf + 2 :]
    acc_ref = None
    if not first:
        acc_ref, refs = refs[0], refs[1:]
    step = pl.program_id(0)
    kept = slots * BLK // 2
    for lane in range(LANES):
        at = slice(lane * BLK, (lane + 1) * BLK)
        hidden = keep_ref[0, :, at] + got_ref[0, :, at].astype(jnp.float32)
        d_act = keep_ref[1, :, at] + got_ref[1, :, at].astype(jnp.float32)
        square = hidden * hidden
        tanh = jnp.tanh(SCALE * (hidden + CUBIC * square * hidden))
        half_up = 0.5 * (1.0 + tanh)
        act = hidden * half_up
        slope = half_up + (0.5 * hidden) * (1.0 - tanh * tanh) * (SCALE + (3.0 * CUBIC * SCALE) * square)
        rights = ((d_act * slope).astype(jnp.bfloat16), act.astype(jnp.bfloat16))
        for side in range(2):
            left = picked_rows(table, buffers, side, step * LANES + lane, slots)
            total = lax.dot_general(
                left, rights[side], (((0,), (0,)), ((), ())), preferred_element_type=jnp.float32
            )
            if not first:
                total = total + acc_ref[side, :, at]
            if last:
                refs[side][:, at] = total[:kept].astype(jnp.bfloat16)
                refs[2][side, :, at] = total[kept:].astype(jnp.bfloat16)
            else:
                refs[0][side, :, at] = total


def grad(table, buffers, keep, got, acc, last):
    tokens, half = keep.shape[1:]
    wide = LANES * BLK
    steps = half // wide
    core_at = table.shape[0] - 1
    slots = core_at // (half // BLK) // 2
    kept = slots * BLK // 2
    whole = [pl.BlockSpec(b.shape, lambda g, t: (0, 0, 0)) for b in buffers]
    mixed = pl.BlockSpec((2, tokens, wide), lambda g, t: (0, 0, g))
    sums = pl.BlockSpec((2, 2 * kept, wide), lambda g, t: (0, 0, g))
    if last:
        own = pl.BlockSpec((kept, wide), lambda g, t: (0, t[core_at] * steps + g))
        out_specs = [own, own, pl.BlockSpec((2, kept, wide), lambda g, t: (0, 0, g))]
        out_shape = [jax.ShapeDtypeStruct((kept, 2 * half), jnp.bfloat16)] * 2 + [
            jax.ShapeDtypeStruct((2, kept, half), jnp.bfloat16)
        ]
    else:
        out_specs = [sums]
        out_shape = [jax.ShapeDtypeStruct((2, 2 * kept, half), jnp.float32)]
    first = acc is None
    return pl.pallas_call(
        functools.partial(grad_kernel, len(buffers), slots, first, last),
        grid_spec=pltpu.PrefetchScalarGridSpec(
            num_scalar_prefetch=1,
            grid=(steps,),
            in_specs=whole + [mixed, mixed] + ([] if first else [sums]),
            out_specs=out_specs,
        ),
        out_shape=out_shape,
        compiler_params=pltpu.CompilerParams(vmem_limit_bytes=VMEM_LIMIT),
        cost_estimate=pl.CostEstimate(flops=1000, bytes_accessed=1000, transcendentals=0),
        name="grad_last" if last else "grad",
    )(table, *buffers, keep, got, *(() if first else (acc,)))


def place_kernel(core, got_ref, in_ref, out_ref, in_out, out_out):
    in_out[...] = got_ref[0]
    out_out[...] = got_ref[1]


def place(core, got, g_in, g_out):
    kept, half = got.shape[1:]
    steps = half // (LANES * BLK)
    anywhere = pl.BlockSpec(memory_space=pl.ANY)
    theirs = pl.BlockSpec((kept, LANES * BLK), lambda g, c: (0, (1 - c[0]) * steps + g))
    return pl.pallas_call(
        place_kernel,
        grid_spec=pltpu.PrefetchScalarGridSpec(
            num_scalar_prefetch=1,
            grid=(steps,),
            in_specs=[pl.BlockSpec((2, kept, LANES * BLK), lambda g, c: (0, 0, g)), anywhere, anywhere],
            out_specs=[theirs, theirs],
        ),
        out_shape=[jax.ShapeDtypeStruct(g_in.shape, g_in.dtype)] * 2,
        input_output_aliases={2: 0, 3: 1},
        name="place",
    )(core, got, g_in, g_out)


def fast(inputs, cotangent, w_in, w_out, keep_in, keep_out):
    kept, width = w_in.shape
    half = width // 2
    here = half // BLK
    mine = kept // BLK
    row = lax.axis_index("row")
    col = lax.axis_index("col")
    core, x = row % 2, row // 2
    z = col // 2
    low = z < 2

    over_x = [(r, r ^ 2) for r in range(ROWS)]
    over_core = [(r, r ^ 1) for r in range(ROWS)]
    over_y = [(c, c ^ 1) for c in range(COLS)]

    def swap_x(v):
        return lax.ppermute(v, "row", over_x)

    def swap_core(v):
        return lax.ppermute(v, "row", over_core)

    def swap_y(v):
        return lax.ppermute(v, "col", over_y)

    def up(v, start):
        return lax.ppermute(v, "col", [(c, c + 2) for c in range(2 * start, COLS - 2)])

    def down(v, start):
        return lax.ppermute(v, "col", [(c + 2, c) for c in range(COLS - 2 - 2 * start)])

    gate = lax.optimization_barrier
    own = jnp.stack((inputs, cotangent), 0)
    other = swap_x(own)

    first = col * 2 * here + core * here
    pieces = []
    for keep in (keep_in, keep_out):
        rows = lax.dynamic_slice_in_dim(keep, first, here, 0)
        pieces.append(
            jnp.concatenate(
                [lax.dynamic_slice_in_dim(rows, r * mine, mine, 1) for r in (row, row ^ 1)], axis=1
            )
        )
    table = jnp.concatenate((jnp.stack(pieces, 1).reshape(-1), core.reshape(1).astype(jnp.int32)))

    s_in, s_out = (
        swap_core(lax.dynamic_slice_in_dim(w, (1 - core) * half, half, 1)) for w in (w_in, w_out)
    )
    other, table, s_in, s_out = gate((other, table, s_in, s_out))

    lead = x == 0
    m0 = jnp.concatenate((jnp.where(lead, own, other), jnp.where(lead, other, own)), axis=1)

    def work(tokens):
        return partial(table, tokens, w_in, w_out, s_in, s_out, core)

    u1, d1, y0, c0 = up(m0, 0), down(m0, 0), swap_y(m0), swap_core(m0)
    u1, d1, y0, c0, m0 = gate((u1, d1, y0, c0, m0))
    m1 = jnp.where(low, d1, u1)
    u2, d2, y1, c1, cy0 = up(u1, 1), down(d1, 1), swap_y(m1), swap_core(m1), swap_core(y0)
    tok0 = (m0, y0, c0, cy0)
    keep0, send0 = work(tok0)
    u2, d2, y1, c1, m1, keep0, send0 = gate((u2, d2, y1, c1, m1, keep0, send0))
    m2 = jnp.where(low, d2, u2)
    u3, d3, y2, c2, cy1, got0 = up(u2, 2), down(d2, 2), swap_y(m2), swap_core(m2), swap_core(y1), swap_x(send0)
    tok1 = (m1, y1, c1, cy1)
    keep1, send1 = work(tok1)
    u3, d3, y2, c2, m2, keep1, send1, got0 = gate((u3, d3, y2, c2, m2, keep1, send1, got0))
    m3 = jnp.where(z == 0, d3, jnp.where(z == 1, u1, jnp.where(z == 2, d1, u3)))
    y3, c3, cy2, got1 = swap_y(m3), swap_core(m3), swap_core(y2), swap_x(send1)
    tok2 = (m2, y2, c2, cy2)
    keep2, send2 = work(tok2)
    (acc,) = grad(table, tok0, keep0, got0, None, False)
    y3, c3, m3, keep2, send2, got1, acc = gate((y3, c3, m3, keep2, send2, got1, acc))
    got2, cy3 = swap_x(send2), swap_core(y3)
    tok3 = (m3, y3, c3, cy3)
    keep3, send3 = work(tok3)
    (acc,) = grad(table, tok1, keep1, got1, acc, False)
    got2, keep3, send3, acc = gate((got2, keep3, send3, acc))
    got3 = swap_x(send3)
    (acc,) = grad(table, tok2, keep2, got2, acc, False)
    got3, acc = gate((got3, acc))
    g_in, g_out, away = grad(table, tok3, keep3, got3, acc, True)
    return tuple(place(core.reshape(1).astype(jnp.int32), swap_core(away), g_in, g_out))


def solution(mesh):
    def per_device(inputs, cotangent, w_in, w_out, keep_in, keep_out):
        kept, width = w_in.shape
        fits = kept % BLK == 0 and width % (2 * LANES * BLK) == 0 and inputs.shape[0] % 16 == 0
        chosen = fast if fits and mesh.shape["row"] == ROWS and mesh.shape["col"] == COLS else general
        return chosen(inputs, cotangent, w_in, w_out, keep_in, keep_out)

    in_specs = (
        P(("row", "col"), None),
        P(("row", "col"), None),
        P("row", "col"),
        P("row", "col"),
        P(),
        P(),
    )
    out_specs = (P("row", "col"), P("row", "col"))
    return jax.shard_map(
        per_device, mesh=mesh, in_specs=in_specs, out_specs=out_specs, check_vma=False
    )
```

```python
import functools

import jax
import jax.numpy as jnp
from jax import lax
from jax.experimental import pallas as pl
from jax.experimental.pallas import tpu as pltpu
from jax.sharding import PartitionSpec as P

D = 6144
BLK = 128
KEEP = 12
ROWS = 4
COLS = 8
LANES = 4
SCALE = 0.7978845608028654
CUBIC = 0.044715
PARTIAL_VMEM = 20 * 1024 * 1024
GRAD_VMEM = 24 * 1024 * 1024
TOTAL_VMEM = 12 * 1024 * 1024
TOTAL_LANES = 6
COST = pl.CostEstimate(flops=0, bytes_accessed=0, transcendentals=0)


def gelu_tanh(values):
    return jax.nn.gelu(values, approximate=True)


def pick_one(matrix, chosen):
    return jnp.take(matrix, chosen, axis=1)


def general(inputs, cotangent, w_in, w_out, keep_in, keep_out):
    width = w_in.shape[1]
    blocks_here = width // BLK
    kept_rows = w_in.shape[0]
    column = lax.axis_index("col")
    own_in = lax.dynamic_slice_in_dim(keep_in, column * blocks_here, blocks_here, 0)
    own_out = lax.dynamic_slice_in_dim(keep_out, column * blocks_here, blocks_here, 0)
    tables = jnp.stack((own_in, own_out), 0)
    stacked = jnp.stack((inputs, cotangent), 0)
    whole = lax.all_gather(stacked, "col", axis=1, tiled=True)
    tokens_here = whole.shape[1]
    blocks = whole.reshape(2, tokens_here, D // BLK, BLK)
    picked = jax.vmap(pick_one)(blocks, tables).reshape(2, tokens_here, blocks_here, KEEP * BLK)
    weights = jnp.stack((w_in, w_out), 1)
    full = lax.all_gather(weights, "row", axis=0, tiled=True)
    panel = full.reshape(KEEP * BLK, 2, blocks_here, BLK)
    mixed = jnp.einsum("ptck,kpcq->ptcq", picked, panel, preferred_element_type=jnp.float32)
    hidden = mixed[0].reshape(tokens_here, width)
    d_act = mixed[1].reshape(tokens_here, width)
    act, pullback = jax.vjp(gelu_tanh, hidden)
    d_hidden = pullback(d_act)[0].astype(jnp.bfloat16)
    act = act.astype(jnp.bfloat16)
    paired = jnp.stack((d_hidden, act), 0).reshape(2, tokens_here, blocks_here, BLK)
    term = jnp.einsum("ptck,ptcq->kpcq", picked, paired, preferred_element_type=jnp.float32)
    summed = (
        lax.psum_scatter(
            term.reshape(lax.axis_size("row") * kept_rows, 2 * width).astype(jnp.bfloat16),
            "row",
            scatter_dimension=0,
            tiled=True,
        )
        .astype(jnp.float32)
        .reshape(kept_rows, 2, width)
    )
    return (summed[:, 0].astype(jnp.bfloat16), summed[:, 1].astype(jnp.bfloat16))


def picked_rows(table, buffers, side, block, slots):
    columns = []
    for slot in range(slots):
        start = pl.multiple_of(table[(block * 2 + side) * slots + slot] * BLK, BLK)
        columns.append(jnp.concatenate([buf[side, :, pl.ds(start, BLK)] for buf in buffers], axis=0))
    return jnp.concatenate(columns, axis=1)


def fixed(array):
    return pl.BlockSpec(array.shape, lambda g, t: (0,) * array.ndim)


def partial_kernel(n_buf, slots, base, table, *refs):
    buffers = refs[:n_buf]
    own = refs[n_buf : n_buf + 2]
    sib = refs[n_buf + 2 : n_buf + 4]
    keep_ref, send_ref = refs[n_buf + 4 :]
    step = pl.program_id(0)
    for lane in range(LANES):
        at = slice(lane * BLK, (lane + 1) * BLK)
        for side in range(2):
            left = picked_rows(table, buffers, side, base + step * LANES + lane, slots)
            right = jnp.concatenate((own[side][:, at], sib[side][:, at]), axis=0)
            total = jnp.dot(left, right, preferred_element_type=jnp.float32)
            keep_ref[side, :, at] = total
            send_ref[side, :, at] = total.astype(jnp.bfloat16)


def partial(table, buffers, weights, part=0, parts=1):
    tokens = sum(b.shape[1] for b in buffers)
    kept, width = weights[0].shape
    wide = LANES * BLK
    steps = width // wide // parts
    weight = pl.BlockSpec((kept, wide), lambda g, t: (0, part * steps + g))
    out = pl.BlockSpec((2, tokens, wide), lambda g, t: (0, 0, g))
    return pl.pallas_call(
        functools.partial(partial_kernel, len(buffers), 2 * kept // BLK, part * steps * LANES),
        grid_spec=pltpu.PrefetchScalarGridSpec(
            num_scalar_prefetch=1,
            grid=(steps,),
            in_specs=[fixed(b) for b in buffers] + [weight] * 4,
            out_specs=[out, out],
        ),
        out_shape=[
            jax.ShapeDtypeStruct((2, tokens, width // parts), dtype) for dtype in (jnp.float32, jnp.bfloat16)
        ],
        compiler_params=pltpu.CompilerParams(vmem_limit_bytes=PARTIAL_VMEM),
        cost_estimate=COST,
        name="partial",
    )(table, *buffers, *weights)


def grad_kernel(units, n_buf, n_keep, n_got, slots, base, table, *refs):
    buffers = refs[:n_buf]
    keeps = refs[n_buf : n_buf + n_keep]
    gots = refs[n_buf + n_keep : n_buf + n_keep + n_got]
    own_ref, away_ref = refs[n_buf + n_keep + n_got :]
    step = pl.program_id(0)
    kept = slots * BLK // 2
    rows = 2 * buffers[0].shape[1]
    for lane in range(LANES):
        at = slice(lane * BLK, (lane + 1) * BLK)

        def gathered(side):
            mine, theirs = [], []
            for keep, keep_at, got, got_at in units:
                mine.append(keeps[keep][side, keep_at * rows : (keep_at + 1) * rows, at])
                theirs.append(gots[got][side, got_at * rows : (got_at + 1) * rows, at])
            return jnp.concatenate(mine, axis=0) + jnp.concatenate(theirs, axis=0).astype(jnp.float32)

        hidden, d_act = gathered(0), gathered(1)
        square = hidden * hidden
        tanh = jnp.tanh(SCALE * (hidden + CUBIC * square * hidden))
        half_up = 0.5 * (1.0 + tanh)
        act = (hidden * half_up).astype(jnp.bfloat16)
        slope = half_up + (0.5 * hidden) * (1.0 - tanh * tanh) * (SCALE + (3.0 * CUBIC * SCALE) * square)
        d_hidden = (d_act * slope).astype(jnp.bfloat16)
        for side, right in enumerate((d_hidden, act)):
            left = picked_rows(table, buffers, side, base + step * LANES + lane, slots)
            total = lax.dot_general(left, right, (((0,), (0,)), ((), ())), preferred_element_type=jnp.float32)
            total = total.astype(jnp.bfloat16)
            own_ref[side, :, at] = total[:kept]
            away_ref[side, :, at] = total[kept:]


def grad(table, units, buffers, keeps, gots, kept, part, parts):
    width = max(keep.shape[2] for keep in keeps)
    wide = LANES * BLK
    steps = width // wide // parts

    def spec(array):
        first = part * steps if array.shape[2] == width else 0
        return pl.BlockSpec((2, array.shape[1], wide), lambda g, t: (0, 0, first + g))

    out = pl.BlockSpec((2, kept, wide), lambda g, t: (0, 0, g))
    return pl.pallas_call(
        functools.partial(
            grad_kernel, units, len(buffers), len(keeps), len(gots), 2 * kept // BLK, part * steps * LANES
        ),
        grid_spec=pltpu.PrefetchScalarGridSpec(
            num_scalar_prefetch=1,
            grid=(steps,),
            in_specs=[fixed(b) for b in buffers] + [spec(v) for v in (*keeps, *gots)],
            out_specs=[out, out],
        ),
        out_shape=[jax.ShapeDtypeStruct((2, kept, width // parts), jnp.bfloat16)] * 2,
        compiler_params=pltpu.CompilerParams(vmem_limit_bytes=GRAD_VMEM),
        cost_estimate=COST,
        name="grad",
    )(table, *buffers, *keeps, *gots)


def total_kernel(own_ref, got_ref, *refs):
    for side, ref in enumerate(refs[-2:]):
        ref[...] = (own_ref[side].astype(jnp.float32) + got_ref[side].astype(jnp.float32)).astype(ref.dtype)


def total(own, got, before, part, parts):
    kept, width = own.shape[1:]
    wide = TOTAL_LANES * BLK
    steps = width // wide
    source = pl.BlockSpec((2, kept, wide), lambda g: (0, 0, g))
    out = pl.BlockSpec((kept, wide), lambda g: (0, part * steps + g))
    return pl.pallas_call(
        total_kernel,
        grid=(steps,),
        in_specs=[source, source] + [pl.BlockSpec(memory_space=pl.ANY)] * len(before),
        out_specs=[out, out],
        out_shape=[jax.ShapeDtypeStruct((kept, width * parts), jnp.bfloat16)] * 2,
        input_output_aliases={2: 0, 3: 1} if before else {},
        compiler_params=pltpu.CompilerParams(vmem_limit_bytes=TOTAL_VMEM),
        cost_estimate=COST,
        name="total",
    )(own, got, *before)


def fast(inputs, cotangent, w_in, w_out, keep_in, keep_out):
    kept, width = w_in.shape
    here = width // BLK
    mine = kept // BLK
    row = lax.axis_index("row")
    col = lax.axis_index("col")

    def swap_x(v):
        return lax.ppermute(v, "row", [(r, r ^ 2) for r in range(ROWS)])

    def swap_core(v):
        return lax.ppermute(v, "row", [(r, r ^ 1) for r in range(ROWS)])

    def swap_y(v):
        return lax.ppermute(v, "col", [(c, c ^ 1) for c in range(COLS)])

    def near(v):
        return lax.ppermute(v, "col", [(c, c ^ 2) for c in range(COLS)])

    def far(v):
        return lax.ppermute(v, "col", [(c, c ^ 4) for c in range(COLS)])

    gate = lax.optimization_barrier

    a0 = jnp.stack((inputs, cotangent), 0)
    b0 = swap_x(a0)
    ya0 = swap_y(a0)
    a1 = near(a0)
    a2 = far(a0)
    s_in = swap_core(w_in)
    pieces = []
    for keep in (keep_in, keep_out):
        rows = lax.dynamic_slice_in_dim(keep, col * here, here, 0)
        pieces += [lax.dynamic_slice_in_dim(rows, r * mine, mine, 1) for r in (row, row ^ 1)]
    table = jnp.concatenate(pieces, axis=1).reshape(-1)
    b0, ya0, a1, a0, s_in, table, w_late = gate((b0, ya0, a1, a0, s_in, table, w_out))
    s_out = swap_core(w_late)
    yb0 = swap_y(b0)
    b1 = near(b0)
    b2 = far(b0)
    s_out, a1 = gate((s_out, a1))
    weights = (w_in, w_out, s_in, s_out)
    ya1 = swap_y(a1)
    keep0, send0 = partial(table, (a0, ya0), weights)
    yb0, a2, send0, b0 = gate((yb0, a2, send0, b0))
    got0 = swap_x(send0)
    ya2 = swap_y(a2)
    a3 = near(a2)
    keep1, send1 = partial(table, (b0, yb0), weights)
    ya1, b1, send1 = gate((ya1, b1, send1))
    got1 = swap_x(send1)
    yb1 = swap_y(b1)
    ya2, b2, a1, a2, ya1 = gate((ya2, b2, a1, a2, ya1))
    b3 = near(b2)
    keep2, send2 = partial(table, (a1, ya1, a2, ya2), weights)
    yb1, a3, send2, got0 = gate((yb1, a3, send2, got0))
    got2 = swap_x(send2)
    ya3 = swap_y(a3)
    yb2 = swap_y(b2)
    ya3, b3, got1, b1, yb1, a3 = gate((ya3, b3, got1, b1, yb1, a3))
    yb3 = swap_y(b3)
    keep3, send3 = partial(table, (b1, yb1, a3, ya3), weights)
    yb2, send3, b2 = gate((yb2, send3, b2))
    got3 = swap_x(send3)
    keep4, send4 = partial(table, (b2, yb2), weights)
    yb3, send4, got2, b3 = gate((yb3, send4, got2, b3))
    got4 = swap_x(send4)
    keep5, send5 = partial(table, (b3, yb3), weights, 0, 2)
    send5, got3, b3, yb3 = gate((send5, got3, b3, yb3))
    got5 = swap_x(send5)
    keep6, send6 = partial(table, (b3, yb3), weights, 1, 2)
    got6 = swap_x(send6)

    buffers = (a0, ya0, b0, yb0, a1, ya1, a2, ya2, b1, yb1, a3, ya3, b2, yb2, b3, yb3)
    units = ((0, 0, 1, 0), (1, 0, 0, 0), (2, 0, 3, 0), (2, 1, 4, 0), (3, 0, 2, 0), (3, 1, 5, 0), (4, 0, 2, 1), (5, 0, 3, 1))
    keeps = (keep0, keep1, keep2, keep3, keep4)
    gots = (got0, got1, got2, got3, got4)
    own0, away0 = grad(table, units, buffers, (*keeps, keep5), (*gots, got5), kept, 0, 2)
    own0, away0, got6 = gate((own0, away0, got6))
    back0 = swap_core(away0)
    own1, away1 = grad(table, units, buffers, (*keeps, keep6), (*gots, got6), kept, 1, 2)
    own1, away1, back0 = gate((own1, away1, back0))
    back1 = swap_core(away1)
    outs = total(own0, back0, (), 0, 2)
    return tuple(total(own1, back1, tuple(outs), 1, 2))


def solution(mesh):
    def per_device(inputs, cotangent, w_in, w_out, keep_in, keep_out):
        kept, width = w_in.shape
        fits = kept % BLK == 0 and inputs.shape[0] % 16 == 0
        fits = fits and all(width % (2 * lanes * BLK) == 0 for lanes in (LANES, TOTAL_LANES))
        chosen = fast if fits and mesh.shape["row"] == ROWS and mesh.shape["col"] == COLS else general
        return chosen(inputs, cotangent, w_in, w_out, keep_in, keep_out)

    in_specs = (
        P(("row", "col"), None),
        P(("row", "col"), None),
        P("row", "col"),
        P("row", "col"),
        P(),
        P(),
    )
    out_specs = (P("row", "col"), P("row", "col"))
    return jax.shard_map(
        per_device, mesh=mesh, in_specs=in_specs, out_specs=out_specs, check_vma=False
    )
```

```python
import functools

import jax
import jax.numpy as jnp
from jax import lax
from jax.experimental import pallas as pl
from jax.experimental.pallas import tpu as pltpu
from jax.sharding import PartitionSpec as P

D = 6144
BLK = 128
KEEP = 12
ROWS = 4
COLS = 8
LANES = 4
SCALE = 0.7978845608028654
CUBIC = 0.044715
PARTIAL_VMEM = 8 * 1024 * 1024
GRAD_VMEM = 16 * 1024 * 1024
TOTAL_VMEM = 8 * 1024 * 1024
PACK_LANES = 4
PACK_VMEM = 12 * 1024 * 1024
TOTAL_LANES = 6
COST = pl.CostEstimate(flops=0, bytes_accessed=0, transcendentals=0)


def gelu_tanh(values):
    return jax.nn.gelu(values, approximate=True)


def pick_one(matrix, chosen):
    return jnp.take(matrix, chosen, axis=1)


def general(inputs, cotangent, w_in, w_out, keep_in, keep_out):
    width = w_in.shape[1]
    blocks_here = width // BLK
    kept_rows = w_in.shape[0]
    column = lax.axis_index("col")
    own_in = lax.dynamic_slice_in_dim(keep_in, column * blocks_here, blocks_here, 0)
    own_out = lax.dynamic_slice_in_dim(keep_out, column * blocks_here, blocks_here, 0)
    tables = jnp.stack((own_in, own_out), 0)
    stacked = jnp.stack((inputs, cotangent), 0)
    whole = lax.all_gather(stacked, "col", axis=1, tiled=True)
    tokens_here = whole.shape[1]
    blocks = whole.reshape(2, tokens_here, D // BLK, BLK)
    picked = jax.vmap(pick_one)(blocks, tables).reshape(2, tokens_here, blocks_here, KEEP * BLK)
    weights = jnp.stack((w_in, w_out), 1)
    full = lax.all_gather(weights, "row", axis=0, tiled=True)
    panel = full.reshape(KEEP * BLK, 2, blocks_here, BLK)
    mixed = jnp.einsum("ptck,kpcq->ptcq", picked, panel, preferred_element_type=jnp.float32)
    hidden = mixed[0].reshape(tokens_here, width)
    d_act = mixed[1].reshape(tokens_here, width)
    act, pullback = jax.vjp(gelu_tanh, hidden)
    d_hidden = pullback(d_act)[0].astype(jnp.bfloat16)
    act = act.astype(jnp.bfloat16)
    paired = jnp.stack((d_hidden, act), 0).reshape(2, tokens_here, blocks_here, BLK)
    term = jnp.einsum("ptck,ptcq->kpcq", picked, paired, preferred_element_type=jnp.float32)
    summed = (
        lax.psum_scatter(
            term.reshape(lax.axis_size("row") * kept_rows, 2 * width).astype(jnp.bfloat16),
            "row",
            scatter_dimension=0,
            tiled=True,
        )
        .astype(jnp.float32)
        .reshape(kept_rows, 2, width)
    )
    return (summed[:, 0].astype(jnp.bfloat16), summed[:, 1].astype(jnp.bfloat16))


def picked_rows(table, buffers, side, block, slots):
    columns = []
    for slot in range(slots):
        start = pl.multiple_of(table[(block * 2 + side) * slots + slot] * BLK, BLK)
        columns.append(jnp.concatenate([buf[side, :, pl.ds(start, BLK)] for buf in buffers], axis=0))
    return jnp.concatenate(columns, axis=1)


def fixed(array):
    return pl.BlockSpec(array.shape, lambda g, t: (0,) * array.ndim, pipeline_mode=pl.Buffered(1))


def pack_kernel(*refs):
    for index, ref in enumerate(refs[:-1]):
        refs[-1][index] = ref[...]


def pack(*weights):
    kept, width = weights[0].shape
    wide = PACK_LANES * BLK
    return pl.pallas_call(
        pack_kernel,
        grid=(width // wide,),
        in_specs=[pl.BlockSpec((kept, wide), lambda g: (0, g))] * len(weights),
        out_specs=pl.BlockSpec((len(weights), kept, wide), lambda g: (0, 0, g)),
        out_shape=jax.ShapeDtypeStruct((len(weights), kept, width), weights[0].dtype),
        compiler_params=pltpu.CompilerParams(vmem_limit_bytes=PACK_VMEM),
        cost_estimate=COST,
        name="pack",
    )(*weights)


def partial_kernel(n_buf, slots, base, table, *refs):
    buffers = refs[:n_buf]
    weights, keep_ref, send_ref = refs[n_buf:]
    step = pl.program_id(0)
    for lane in range(LANES):
        at = slice(lane * BLK, (lane + 1) * BLK)
        for side in range(2):
            left = picked_rows(table, buffers, side, base + step * LANES + lane, slots)
            right = jnp.concatenate((weights[side, :, at], weights[2 + side, :, at]), axis=0)
            total = jnp.dot(left, right, preferred_element_type=jnp.float32)
            keep_ref[side, :, at] = total
            send_ref[side, :, at] = total.astype(jnp.bfloat16)


def partial(table, buffers, weights, part=0, parts=1):
    tokens = sum(b.shape[1] for b in buffers)
    kept, width = weights.shape[1:]
    wide = LANES * BLK
    steps = width // wide // parts
    weight = pl.BlockSpec((4, kept, wide), lambda g, t: (0, 0, part * steps + g))
    out = pl.BlockSpec((2, tokens, wide), lambda g, t: (0, 0, g))
    return pl.pallas_call(
        functools.partial(partial_kernel, len(buffers), 2 * kept // BLK, part * steps * LANES),
        grid_spec=pltpu.PrefetchScalarGridSpec(
            num_scalar_prefetch=1,
            grid=(steps,),
            in_specs=[fixed(b) for b in buffers] + [weight],
            out_specs=[out, out],
        ),
        out_shape=[
            jax.ShapeDtypeStruct((2, tokens, width // parts), dtype) for dtype in (jnp.float32, jnp.bfloat16)
        ],
        compiler_params=pltpu.CompilerParams(vmem_limit_bytes=PARTIAL_VMEM),
        cost_estimate=COST,
        name="partial",
    )(table, *buffers, weights)


def grad_kernel(units, n_buf, n_keep, n_got, slots, base, table, *refs):
    buffers = refs[:n_buf]
    keeps = refs[n_buf : n_buf + n_keep]
    gots = refs[n_buf + n_keep : n_buf + n_keep + n_got]
    own_ref, away_ref = refs[n_buf + n_keep + n_got :]
    step = pl.program_id(0)
    kept = slots * BLK // 2
    rows = 2 * buffers[0].shape[1]
    for lane in range(LANES):
        at = slice(lane * BLK, (lane + 1) * BLK)

        def gathered(side):
            mine, theirs = [], []
            for keep, keep_at, got, got_at in units:
                mine.append(keeps[keep][side, keep_at * rows : (keep_at + 1) * rows, at])
                theirs.append(gots[got][side, got_at * rows : (got_at + 1) * rows, at])
            return jnp.concatenate(mine, axis=0) + jnp.concatenate(theirs, axis=0).astype(jnp.float32)

        hidden, d_act = gathered(0), gathered(1)
        square = hidden * hidden
        tanh = jnp.tanh(SCALE * (hidden + CUBIC * square * hidden))
        half_up = 0.5 * (1.0 + tanh)
        act = (hidden * half_up).astype(jnp.bfloat16)
        slope = half_up + (0.5 * hidden) * (1.0 - tanh * tanh) * (SCALE + (3.0 * CUBIC * SCALE) * square)
        d_hidden = (d_act * slope).astype(jnp.bfloat16)
        for side, right in enumerate((d_hidden, act)):
            left = picked_rows(table, buffers, side, base + step * LANES + lane, slots)
            total = lax.dot_general(left, right, (((0,), (0,)), ((), ())), preferred_element_type=jnp.float32)
            total = total.astype(jnp.bfloat16)
            own_ref[side, :, at] = total[:kept]
            away_ref[side, :, at] = total[kept:]


def grad(table, units, buffers, keeps, gots, kept, part, parts):
    width = max(keep.shape[2] for keep in keeps)
    wide = LANES * BLK
    steps = width // wide // parts

    def spec(array):
        first = part * steps if array.shape[2] == width else 0
        return pl.BlockSpec((2, array.shape[1], wide), lambda g, t: (0, 0, first + g))

    out = pl.BlockSpec((2, kept, wide), lambda g, t: (0, 0, g))
    return pl.pallas_call(
        functools.partial(
            grad_kernel, units, len(buffers), len(keeps), len(gots), 2 * kept // BLK, part * steps * LANES
        ),
        grid_spec=pltpu.PrefetchScalarGridSpec(
            num_scalar_prefetch=1,
            grid=(steps,),
            in_specs=[fixed(b) for b in buffers] + [spec(v) for v in (*keeps, *gots)],
            out_specs=[out, out],
        ),
        out_shape=[jax.ShapeDtypeStruct((2, kept, width // parts), jnp.bfloat16)] * 2,
        compiler_params=pltpu.CompilerParams(vmem_limit_bytes=GRAD_VMEM),
        cost_estimate=COST,
        name="grad",
    )(table, *buffers, *keeps, *gots)


def total_kernel(own_ref, got_ref, *refs):
    for side, ref in enumerate(refs[-2:]):
        ref[...] = (own_ref[side].astype(jnp.float32) + got_ref[side].astype(jnp.float32)).astype(ref.dtype)


def total(own, got, before, part, parts):
    kept, width = own.shape[1:]
    wide = TOTAL_LANES * BLK
    steps = width // wide
    source = pl.BlockSpec((2, kept, wide), lambda g: (0, 0, g))
    out = pl.BlockSpec((kept, wide), lambda g: (0, part * steps + g))
    return pl.pallas_call(
        total_kernel,
        grid=(steps,),
        in_specs=[source, source] + [pl.BlockSpec(memory_space=pl.ANY)] * len(before),
        out_specs=[out, out],
        out_shape=[jax.ShapeDtypeStruct((kept, width * parts), jnp.bfloat16)] * 2,
        input_output_aliases={2: 0, 3: 1} if before else {},
        compiler_params=pltpu.CompilerParams(vmem_limit_bytes=TOTAL_VMEM),
        cost_estimate=COST,
        name="total",
    )(own, got, *before)


def fast(inputs, cotangent, w_in, w_out, keep_in, keep_out):
    kept, width = w_in.shape
    here = width // BLK
    mine = kept // BLK
    row = lax.axis_index("row")
    col = lax.axis_index("col")

    def swap_x(v):
        return lax.ppermute(v, "row", [(r, r ^ 2) for r in range(ROWS)])

    def swap_core(v):
        return lax.ppermute(v, "row", [(r, r ^ 1) for r in range(ROWS)])

    def swap_y(v):
        return lax.ppermute(v, "col", [(c, c ^ 1) for c in range(COLS)])

    def near(v):
        return lax.ppermute(v, "col", [(c, c ^ 2) for c in range(COLS)])

    def far(v):
        return lax.ppermute(v, "col", [(c, c ^ 4) for c in range(COLS)])

    gate = lax.optimization_barrier

    a0 = jnp.stack((inputs, cotangent), 0)
    b0, ya0, a1 = swap_x(a0), swap_y(a0), near(a0)
    s_in, s_out = swap_core(w_in), swap_core(w_out)
    pieces = []
    for keep in (keep_in, keep_out):
        rows = lax.dynamic_slice_in_dim(keep, col * here, here, 0)
        pieces += [lax.dynamic_slice_in_dim(rows, r * mine, mine, 1) for r in (row, row ^ 1)]
    table = jnp.concatenate(pieces, axis=1).reshape(-1)
    weights = pack(w_in, w_out, s_in, s_out)
    table, weights, b0, ya0, a1, a0 = gate((table, weights, b0, ya0, a1, a0))
    yb0, b1, ya1, a2 = swap_y(b0), near(b0), swap_y(a1), far(a0)
    keep0, send0 = partial(table, (a0, ya0), weights)
    table, send0 = gate((table, send0))
    got0 = swap_x(send0)
    table, yb0, b0 = gate((table, yb0, b0))
    keep1, send1 = partial(table, (b0, yb0), weights)
    table, send1, b1 = gate((table, send1, b1))
    got1, yb1 = swap_x(send1), swap_y(b1)
    table, got0, b0 = gate((table, got0, b0))
    b2 = far(b0)
    table, ya1, a1 = gate((table, ya1, a1))
    keep2, send2 = partial(table, (a1, ya1), weights)
    table, send2, a2, got1 = gate((table, send2, a2, got1))
    got2, ya2, a3 = swap_x(send2), swap_y(a2), near(a2)
    table, yb1, b1 = gate((table, yb1, b1))
    keep3, send3 = partial(table, (b1, yb1), weights)
    table, send3 = gate((table, send3))
    got3 = swap_x(send3)
    table, a3 = gate((table, a3))
    ya3 = swap_y(a3)
    table, ya2, got2 = gate((table, ya2, got2))
    keep4, send4 = partial(table, (a2, ya2), weights)
    table, send4, b2 = gate((table, send4, b2))
    got4, yb2, b3 = swap_x(send4), swap_y(b2), near(b2)
    table, ya3, got3 = gate((table, ya3, got3))
    keep5, send5 = partial(table, (a3, ya3), weights)
    table, send5 = gate((table, send5))
    got5 = swap_x(send5)
    table, b3 = gate((table, b3))
    yb3 = swap_y(b3)
    table, yb2, got4 = gate((table, yb2, got4))
    keep6, send6 = partial(table, (b2, yb2), weights)
    table, send6 = gate((table, send6))
    got6 = swap_x(send6)
    table, yb3, got5 = gate((table, yb3, got5))
    keep7, send7 = partial(table, (b3, yb3), weights, 0, 2)
    table, send7 = gate((table, send7))
    got7 = swap_x(send7)
    keep8, send8 = partial(table, (b3, yb3), weights, 1, 2)
    table, send8, got6 = gate((table, send8, got6))
    got8 = swap_x(send8)

    buffers = (a0, ya0, b0, yb0, a1, ya1, b1, yb1, a2, ya2, a3, ya3, b2, yb2, b3, yb3)
    units = ((0, 0, 1, 0), (1, 0, 0, 0), (2, 0, 3, 0), (3, 0, 2, 0), (4, 0, 6, 0), (5, 0, 7, 0), (6, 0, 4, 0), (7, 0, 5, 0))
    keeps = (keep0, keep1, keep2, keep3, keep4, keep5, keep6)
    gots = (got0, got1, got2, got3, got4, got5, got6)
    own0, away0 = grad(table, units, buffers, (*keeps, keep7), (*gots, got7), kept, 0, 2)
    own0, away0, got8 = gate((own0, away0, got8))
    back0 = swap_core(away0)
    own1, away1 = grad(table, units, buffers, (*keeps, keep8), (*gots, got8), kept, 1, 2)
    own1, away1, back0 = gate((own1, away1, back0))
    back1 = swap_core(away1)
    outs = total(own0, back0, (), 0, 2)
    return tuple(total(own1, back1, tuple(outs), 1, 2))


def solution(mesh):
    def per_device(inputs, cotangent, w_in, w_out, keep_in, keep_out):
        kept, width = w_in.shape
        fits = kept % BLK == 0 and inputs.shape[0] % 16 == 0
        fits = fits and all(width % (2 * lanes * BLK) == 0 for lanes in (LANES, TOTAL_LANES))
        chosen = fast if fits and mesh.shape["row"] == ROWS and mesh.shape["col"] == COLS else general
        return chosen(inputs, cotangent, w_in, w_out, keep_in, keep_out)

    in_specs = (
        P(("row", "col"), None),
        P(("row", "col"), None),
        P("row", "col"),
        P("row", "col"),
        P(),
        P(),
    )
    out_specs = (P("row", "col"), P("row", "col"))
    return jax.shard_map(
        per_device, mesh=mesh, in_specs=in_specs, out_specs=out_specs, check_vma=False
    )
```

```python
import functools

import jax
import jax.numpy as jnp
from jax import lax
from jax.experimental import pallas as pl
from jax.experimental.pallas import tpu as pltpu
from jax.sharding import PartitionSpec as P

D = 6144
BLK = 128
KEEP = 12
ROWS = 4
COLS = 8
LANES = 4
SCALE = 0.7978845608028654
CUBIC = 0.044715
PARTIAL_VMEM = 8 * 1024 * 1024
GRAD_VMEM = 16 * 1024 * 1024
TOTAL_VMEM = 8 * 1024 * 1024
PACK_LANES = 4
PACK_VMEM = 12 * 1024 * 1024
TOTAL_LANES = 8
PARTS = 3
COST = pl.CostEstimate(flops=0, bytes_accessed=0, transcendentals=0)


def gelu_tanh(values):
    return jax.nn.gelu(values, approximate=True)


def pick_one(matrix, chosen):
    return jnp.take(matrix, chosen, axis=1)


def general(inputs, cotangent, w_in, w_out, keep_in, keep_out):
    width = w_in.shape[1]
    blocks_here = width // BLK
    kept_rows = w_in.shape[0]
    column = lax.axis_index("col")
    own_in = lax.dynamic_slice_in_dim(keep_in, column * blocks_here, blocks_here, 0)
    own_out = lax.dynamic_slice_in_dim(keep_out, column * blocks_here, blocks_here, 0)
    tables = jnp.stack((own_in, own_out), 0)
    stacked = jnp.stack((inputs, cotangent), 0)
    whole = lax.all_gather(stacked, "col", axis=1, tiled=True)
    tokens_here = whole.shape[1]
    blocks = whole.reshape(2, tokens_here, D // BLK, BLK)
    picked = jax.vmap(pick_one)(blocks, tables).reshape(2, tokens_here, blocks_here, KEEP * BLK)
    weights = jnp.stack((w_in, w_out), 1)
    full = lax.all_gather(weights, "row", axis=0, tiled=True)
    panel = full.reshape(KEEP * BLK, 2, blocks_here, BLK)
    mixed = jnp.einsum("ptck,kpcq->ptcq", picked, panel, preferred_element_type=jnp.float32)
    hidden = mixed[0].reshape(tokens_here, width)
    d_act = mixed[1].reshape(tokens_here, width)
    act, pullback = jax.vjp(gelu_tanh, hidden)
    d_hidden = pullback(d_act)[0].astype(jnp.bfloat16)
    act = act.astype(jnp.bfloat16)
    paired = jnp.stack((d_hidden, act), 0).reshape(2, tokens_here, blocks_here, BLK)
    term = jnp.einsum("ptck,ptcq->kpcq", picked, paired, preferred_element_type=jnp.float32)
    summed = (
        lax.psum_scatter(
            term.reshape(lax.axis_size("row") * kept_rows, 2 * width).astype(jnp.bfloat16),
            "row",
            scatter_dimension=0,
            tiled=True,
        )
        .astype(jnp.float32)
        .reshape(kept_rows, 2, width)
    )
    return (summed[:, 0].astype(jnp.bfloat16), summed[:, 1].astype(jnp.bfloat16))


def picked_rows(table, buffers, side, block, slots):
    columns = []
    for slot in range(slots):
        start = pl.multiple_of(table[(block * 2 + side) * slots + slot] * BLK, BLK)
        columns.append(jnp.concatenate([buf[side, :, pl.ds(start, BLK)] for buf in buffers], axis=0))
    return jnp.concatenate(columns, axis=1)


def fixed(array):
    return pl.BlockSpec(array.shape, lambda g, t: (0,) * array.ndim, pipeline_mode=pl.Buffered(1))


def pack_kernel(*refs):
    for index, ref in enumerate(refs[:-1]):
        refs[-1][index] = ref[...]


def pack(*weights):
    kept, width = weights[0].shape
    wide = PACK_LANES * BLK
    return pl.pallas_call(
        pack_kernel,
        grid=(width // wide,),
        in_specs=[pl.BlockSpec((kept, wide), lambda g: (0, g))] * len(weights),
        out_specs=pl.BlockSpec((len(weights), kept, wide), lambda g: (0, 0, g)),
        out_shape=jax.ShapeDtypeStruct((len(weights), kept, width), weights[0].dtype),
        compiler_params=pltpu.CompilerParams(vmem_limit_bytes=PACK_VMEM),
        cost_estimate=COST,
        name="pack",
    )(*weights)


def partial_kernel(n_buf, slots, base, table, *refs):
    buffers = refs[:n_buf]
    weights, keep_ref, send_ref = refs[n_buf:]
    step = pl.program_id(0)
    for lane in range(LANES):
        at = slice(lane * BLK, (lane + 1) * BLK)
        for side in range(2):
            left = picked_rows(table, buffers, side, base + step * LANES + lane, slots)
            right = jnp.concatenate((weights[side, :, at], weights[2 + side, :, at]), axis=0)
            total = jnp.dot(left, right, preferred_element_type=jnp.float32)
            keep_ref[side, :, at] = total
            send_ref[side, :, at] = total.astype(jnp.bfloat16)


def partial(table, buffers, weights, part=0, parts=1):
    tokens = sum(b.shape[1] for b in buffers)
    kept, width = weights.shape[1:]
    wide = LANES * BLK
    steps = width // wide // parts
    weight = pl.BlockSpec((4, kept, wide), lambda g, t: (0, 0, part * steps + g))
    out = pl.BlockSpec((2, tokens, wide), lambda g, t: (0, 0, g))
    return pl.pallas_call(
        functools.partial(partial_kernel, len(buffers), 2 * kept // BLK, part * steps * LANES),
        grid_spec=pltpu.PrefetchScalarGridSpec(
            num_scalar_prefetch=1,
            grid=(steps,),
            in_specs=[fixed(b) for b in buffers] + [weight],
            out_specs=[out, out],
        ),
        out_shape=[
            jax.ShapeDtypeStruct((2, tokens, width // parts), dtype) for dtype in (jnp.float32, jnp.bfloat16)
        ],
        compiler_params=pltpu.CompilerParams(vmem_limit_bytes=PARTIAL_VMEM),
        cost_estimate=COST,
        name="partial",
    )(table, *buffers, weights)


def grad_kernel(units, n_buf, n_keep, n_got, slots, base, table, *refs):
    buffers = refs[:n_buf]
    keeps = refs[n_buf : n_buf + n_keep]
    gots = refs[n_buf + n_keep : n_buf + n_keep + n_got]
    own_ref, away_ref = refs[n_buf + n_keep + n_got :]
    step = pl.program_id(0)
    kept = slots * BLK // 2
    rows = 2 * buffers[0].shape[1]
    for lane in range(LANES):
        at = slice(lane * BLK, (lane + 1) * BLK)

        def gathered(side):
            mine, theirs = [], []
            for keep, keep_at, got, got_at in units:
                mine.append(keeps[keep][side, keep_at * rows : (keep_at + 1) * rows, at])
                theirs.append(gots[got][side, got_at * rows : (got_at + 1) * rows, at])
            return jnp.concatenate(mine, axis=0) + jnp.concatenate(theirs, axis=0).astype(jnp.float32)

        hidden, d_act = gathered(0), gathered(1)
        square = hidden * hidden
        tanh = jnp.tanh(SCALE * (hidden + CUBIC * square * hidden))
        half_up = 0.5 * (1.0 + tanh)
        act = (hidden * half_up).astype(jnp.bfloat16)
        slope = half_up + (0.5 * hidden) * (1.0 - tanh * tanh) * (SCALE + (3.0 * CUBIC * SCALE) * square)
        d_hidden = (d_act * slope).astype(jnp.bfloat16)
        for side, right in enumerate((d_hidden, act)):
            left = picked_rows(table, buffers, side, base + step * LANES + lane, slots)
            total = lax.dot_general(left, right, (((0,), (0,)), ((), ())), preferred_element_type=jnp.float32)
            total = total.astype(jnp.bfloat16)
            own_ref[side, :, at] = total[:kept]
            away_ref[side, :, at] = total[kept:]


def grad(table, units, buffers, keeps, gots, kept, part, parts):
    width = max(keep.shape[2] for keep in keeps)
    wide = LANES * BLK
    steps = width // wide // parts

    def spec(array):
        first = part * steps if array.shape[2] == width else 0
        return pl.BlockSpec((2, array.shape[1], wide), lambda g, t: (0, 0, first + g))

    out = pl.BlockSpec((2, kept, wide), lambda g, t: (0, 0, g))
    return pl.pallas_call(
        functools.partial(
            grad_kernel, units, len(buffers), len(keeps), len(gots), 2 * kept // BLK, part * steps * LANES
        ),
        grid_spec=pltpu.PrefetchScalarGridSpec(
            num_scalar_prefetch=1,
            grid=(steps,),
            in_specs=[fixed(b) for b in buffers] + [spec(v) for v in (*keeps, *gots)],
            out_specs=[out, out],
        ),
        out_shape=[jax.ShapeDtypeStruct((2, kept, width // parts), jnp.bfloat16)] * 2,
        compiler_params=pltpu.CompilerParams(vmem_limit_bytes=GRAD_VMEM),
        cost_estimate=COST,
        name="grad",
    )(table, *buffers, *keeps, *gots)


def total_kernel(own_ref, got_ref, *refs):
    for side, ref in enumerate(refs[-2:]):
        ref[...] = (own_ref[side].astype(jnp.float32) + got_ref[side].astype(jnp.float32)).astype(ref.dtype)


def total(own, got, before, part, parts):
    kept, width = own.shape[1:]
    wide = TOTAL_LANES * BLK
    steps = width // wide
    source = pl.BlockSpec((2, kept, wide), lambda g: (0, 0, g))
    out = pl.BlockSpec((kept, wide), lambda g: (0, part * steps + g))
    return pl.pallas_call(
        total_kernel,
        grid=(steps,),
        in_specs=[source, source] + [pl.BlockSpec(memory_space=pl.ANY)] * len(before),
        out_specs=[out, out],
        out_shape=[jax.ShapeDtypeStruct((kept, width * parts), jnp.bfloat16)] * 2,
        input_output_aliases={2: 0, 3: 1} if before else {},
        compiler_params=pltpu.CompilerParams(vmem_limit_bytes=TOTAL_VMEM),
        cost_estimate=COST,
        name="total",
    )(own, got, *before)


def fast(inputs, cotangent, w_in, w_out, keep_in, keep_out):
    kept, width = w_in.shape
    here = width // BLK
    mine = kept // BLK
    row = lax.axis_index("row")
    col = lax.axis_index("col")

    def swap_x(v):
        return lax.ppermute(v, "row", [(r, r ^ 2) for r in range(ROWS)])

    def swap_core(v):
        return lax.ppermute(v, "row", [(r, r ^ 1) for r in range(ROWS)])

    def swap_y(v):
        return lax.ppermute(v, "col", [(c, c ^ 1) for c in range(COLS)])

    def near(v):
        return lax.ppermute(v, "col", [(c, c ^ 2) for c in range(COLS)])

    def far(v):
        return lax.ppermute(v, "col", [(c, c ^ 4) for c in range(COLS)])

    gate = lax.optimization_barrier

    a0 = jnp.stack((inputs, cotangent), 0)
    b0, ya0, a1 = swap_x(a0), swap_y(a0), near(a0)
    s_in, s_out = swap_core(w_in), swap_core(w_out)
    pieces = []
    for keep in (keep_in, keep_out):
        rows = lax.dynamic_slice_in_dim(keep, col * here, here, 0)
        pieces += [lax.dynamic_slice_in_dim(rows, r * mine, mine, 1) for r in (row, row ^ 1)]
    table = jnp.concatenate(pieces, axis=1).reshape(-1)
    held = [pltpu.with_memory_space_constraint(w, pltpu.HBM) for w in (w_in, w_out)]
    weights = pack(*held, s_in, s_out)
    table, weights, b0, ya0, a1, a0 = gate((table, weights, b0, ya0, a1, a0))
    yb0, b1, ya1, a2 = swap_y(b0), near(b0), swap_y(a1), far(a0)
    keep0, send0 = partial(table, (a0, ya0), weights)
    table, send0 = gate((table, send0))
    got0 = swap_x(send0)
    table, yb0, b0 = gate((table, yb0, b0))
    keep1, send1 = partial(table, (b0, yb0), weights)
    table, send1 = gate((table, send1))
    got1 = swap_x(send1)
    table, b1 = gate((table, b1))
    yb1 = swap_y(b1)
    table, got0, b0 = gate((table, got0, b0))
    b2 = far(b0)
    table, ya1, a1 = gate((table, ya1, a1))
    keep2, send2 = partial(table, (a1, ya1), weights)
    table, send2, a2, got1 = gate((table, send2, a2, got1))
    got2, ya2, a3 = swap_x(send2), swap_y(a2), near(a2)
    table, yb1, b1 = gate((table, yb1, b1))
    keep3, send3 = partial(table, (b1, yb1), weights)
    table, send3 = gate((table, send3))
    got3 = swap_x(send3)
    table, a3 = gate((table, a3))
    ya3 = swap_y(a3)
    table, ya2, got2 = gate((table, ya2, got2))
    keep4, send4 = partial(table, (a2, ya2), weights)
    table, send4, b2 = gate((table, send4, b2))
    got4, yb2, b3 = swap_x(send4), swap_y(b2), near(b2)
    table, ya3, got3 = gate((table, ya3, got3))
    keep5, send5 = partial(table, (a3, ya3), weights)
    table, send5 = gate((table, send5))
    got5 = swap_x(send5)
    table, b3 = gate((table, b3))
    yb3 = swap_y(b3)
    table, yb2, got4 = gate((table, yb2, got4))
    keep6, send6 = partial(table, (b2, yb2), weights)
    table, send6 = gate((table, send6))
    got6 = swap_x(send6)
    table, yb3, got5 = gate((table, yb3, got5))
    keep7, got7 = [], []
    for part in range(PARTS):
        keep, send = partial(table, (b3, yb3), weights, part, PARTS)
        table, send = gate((table, send))
        keep7.append(keep)
        got7.append(swap_x(send))
    table, got6, got7[0] = gate((table, got6, got7[0]))

    buffers = (a0, ya0, b0, yb0, a1, ya1, b1, yb1, a2, ya2, a3, ya3, b2, yb2, b3, yb3)
    units = ((0, 0, 1, 0), (1, 0, 0, 0), (2, 0, 3, 0), (3, 0, 2, 0), (4, 0, 6, 0), (5, 0, 7, 0), (6, 0, 4, 0), (7, 0, 5, 0))
    keeps = (keep0, keep1, keep2, keep3, keep4, keep5, keep6)
    gots = (got0, got1, got2, got3, got4, got5, got6)
    outs, waiting = (), None
    for part in range(PARTS):
        own, away = grad(table, units, buffers, (*keeps, keep7[part]), (*gots, got7[part]), kept, part, PARTS)
        if part < PARTS - 1:
            table, own, away, got7[part + 1] = gate((table, own, away, got7[part + 1]))
        back = swap_core(away)
        if waiting is not None:
            outs = total(*waiting, outs, part - 1, PARTS)
        waiting = (own, back)
    return tuple(total(*waiting, tuple(outs), PARTS - 1, PARTS))


def solution(mesh):
    def per_device(inputs, cotangent, w_in, w_out, keep_in, keep_out):
        kept, width = w_in.shape
        fits = kept % BLK == 0 and inputs.shape[0] % 16 == 0
        fits = fits and all(width % (PARTS * lanes * BLK) == 0 for lanes in (LANES, PACK_LANES, TOTAL_LANES))
        chosen = fast if fits and mesh.shape["row"] == ROWS and mesh.shape["col"] == COLS else general
        return chosen(inputs, cotangent, w_in, w_out, keep_in, keep_out)

    in_specs = (
        P(("row", "col"), None),
        P(("row", "col"), None),
        P("row", "col"),
        P("row", "col"),
        P(),
        P(),
    )
    out_specs = (P("row", "col"), P("row", "col"))
    return jax.shard_map(
        per_device, mesh=mesh, in_specs=in_specs, out_specs=out_specs, check_vma=False
    )
```

```python
import functools

import jax
import jax.numpy as jnp
from jax import lax
from jax.experimental import pallas as pl
from jax.experimental.pallas import tpu as pltpu
from jax.sharding import PartitionSpec as P

D = 6144
BLK = 128
KEEP = 12
ROWS = 4
COLS = 8
LANES = 4
SCALE = 0.7978845608028654
CUBIC = 0.044715
PARTIAL_VMEM = 8 * 1024 * 1024
GRAD_VMEM = 16 * 1024 * 1024
TOTAL_VMEM = 8 * 1024 * 1024
PACK_LANES = 4
TICK_VMEM = 1024 * 1024
PACK_VMEM = 12 * 1024 * 1024
TOTAL_LANES = 8
PARTS = 3
COST = pl.CostEstimate(flops=0, bytes_accessed=0, transcendentals=0)


def gelu_tanh(values):
    return jax.nn.gelu(values, approximate=True)


def pick_one(matrix, chosen):
    return jnp.take(matrix, chosen, axis=1)


def general(inputs, cotangent, w_in, w_out, keep_in, keep_out):
    width = w_in.shape[1]
    blocks_here = width // BLK
    kept_rows = w_in.shape[0]
    column = lax.axis_index("col")
    own_in = lax.dynamic_slice_in_dim(keep_in, column * blocks_here, blocks_here, 0)
    own_out = lax.dynamic_slice_in_dim(keep_out, column * blocks_here, blocks_here, 0)
    tables = jnp.stack((own_in, own_out), 0)
    stacked = jnp.stack((inputs, cotangent), 0)
    whole = lax.all_gather(stacked, "col", axis=1, tiled=True)
    tokens_here = whole.shape[1]
    blocks = whole.reshape(2, tokens_here, D // BLK, BLK)
    picked = jax.vmap(pick_one)(blocks, tables).reshape(2, tokens_here, blocks_here, KEEP * BLK)
    weights = jnp.stack((w_in, w_out), 1)
    full = lax.all_gather(weights, "row", axis=0, tiled=True)
    panel = full.reshape(KEEP * BLK, 2, blocks_here, BLK)
    mixed = jnp.einsum("ptck,kpcq->ptcq", picked, panel, preferred_element_type=jnp.float32)
    hidden = mixed[0].reshape(tokens_here, width)
    d_act = mixed[1].reshape(tokens_here, width)
    act, pullback = jax.vjp(gelu_tanh, hidden)
    d_hidden = pullback(d_act)[0].astype(jnp.bfloat16)
    act = act.astype(jnp.bfloat16)
    paired = jnp.stack((d_hidden, act), 0).reshape(2, tokens_here, blocks_here, BLK)
    term = jnp.einsum("ptck,ptcq->kpcq", picked, paired, preferred_element_type=jnp.float32)
    summed = (
        lax.psum_scatter(
            term.reshape(lax.axis_size("row") * kept_rows, 2 * width).astype(jnp.bfloat16),
            "row",
            scatter_dimension=0,
            tiled=True,
        )
        .astype(jnp.float32)
        .reshape(kept_rows, 2, width)
    )
    return (summed[:, 0].astype(jnp.bfloat16), summed[:, 1].astype(jnp.bfloat16))


def picked_rows(table, buffers, side, block, slots):
    columns = []
    for slot in range(slots):
        start = pl.multiple_of(table[(block * 2 + side) * slots + slot] * BLK, BLK)
        columns.append(jnp.concatenate([buf[side, :, pl.ds(start, BLK)] for buf in buffers], axis=0))
    return jnp.concatenate(columns, axis=1)


def fixed(array):
    return pl.BlockSpec(array.shape, lambda g, t: (0,) * array.ndim, pipeline_mode=pl.Buffered(1))


def pack_kernel(*refs):
    for index, ref in enumerate(refs[:-1]):
        refs[-1][index] = ref[...]


def pack(*weights):
    kept, width = weights[0].shape
    wide = PACK_LANES * BLK
    return pl.pallas_call(
        pack_kernel,
        grid=(width // wide,),
        in_specs=[pl.BlockSpec((kept, wide), lambda g: (0, g))] * len(weights),
        out_specs=pl.BlockSpec((len(weights), kept, wide), lambda g: (0, 0, g)),
        out_shape=jax.ShapeDtypeStruct((len(weights), kept, width), weights[0].dtype),
        compiler_params=pltpu.CompilerParams(vmem_limit_bytes=PACK_VMEM),
        cost_estimate=COST,
        name="pack",
    )(*weights)


def partial_kernel(n_buf, slots, base, table, *refs):
    buffers = refs[:n_buf]
    weights, keep_ref, send_ref = refs[n_buf:]
    step = pl.program_id(0)
    for lane in range(LANES):
        at = slice(lane * BLK, (lane + 1) * BLK)
        for side in range(2):
            left = picked_rows(table, buffers, side, base + step * LANES + lane, slots)
            right = jnp.concatenate((weights[side, :, at], weights[2 + side, :, at]), axis=0)
            total = jnp.dot(left, right, preferred_element_type=jnp.float32)
            keep_ref[side, :, at] = total
            send_ref[side, :, at] = total.astype(jnp.bfloat16)


def partial(table, buffers, weights, part=0, parts=1):
    tokens = sum(b.shape[1] for b in buffers)
    kept, width = weights.shape[1:]
    wide = LANES * BLK
    steps = width // wide // parts
    weight = pl.BlockSpec((4, kept, wide), lambda g, t: (0, 0, part * steps + g))
    out = pl.BlockSpec((2, tokens, wide), lambda g, t: (0, 0, g))
    return pl.pallas_call(
        functools.partial(partial_kernel, len(buffers), 2 * kept // BLK, part * steps * LANES),
        grid_spec=pltpu.PrefetchScalarGridSpec(
            num_scalar_prefetch=1,
            grid=(steps,),
            in_specs=[fixed(b) for b in buffers] + [weight],
            out_specs=[out, out],
        ),
        out_shape=[
            jax.ShapeDtypeStruct((2, tokens, width // parts), dtype) for dtype in (jnp.float32, jnp.bfloat16)
        ],
        compiler_params=pltpu.CompilerParams(vmem_limit_bytes=PARTIAL_VMEM),
        cost_estimate=COST,
        name="partial",
    )(table, *buffers, weights)


def tick_kernel(table_ref, out_ref):
    pass


def tick(table):
    anywhere = pl.BlockSpec(memory_space=pl.ANY)
    return pl.pallas_call(
        tick_kernel,
        in_specs=[anywhere],
        out_specs=anywhere,
        out_shape=jax.ShapeDtypeStruct(table.shape, table.dtype),
        input_output_aliases={0: 0},
        compiler_params=pltpu.CompilerParams(vmem_limit_bytes=TICK_VMEM),
        cost_estimate=COST,
        name="tick",
    )(table)


def grad_kernel(units, n_buf, n_keep, n_got, slots, base, table, *refs):
    buffers = refs[:n_buf]
    keeps = refs[n_buf : n_buf + n_keep]
    gots = refs[n_buf + n_keep : n_buf + n_keep + n_got]
    own_ref, away_ref = refs[n_buf + n_keep + n_got :]
    step = pl.program_id(0)
    kept = slots * BLK // 2
    rows = 2 * buffers[0].shape[1]
    for lane in range(LANES):
        at = slice(lane * BLK, (lane + 1) * BLK)

        def gathered(side):
            mine, theirs = [], []
            for keep, keep_at, got, got_at in units:
                mine.append(keeps[keep][side, keep_at * rows : (keep_at + 1) * rows, at])
                theirs.append(gots[got][side, got_at * rows : (got_at + 1) * rows, at])
            return jnp.concatenate(mine, axis=0) + jnp.concatenate(theirs, axis=0).astype(jnp.float32)

        hidden, d_act = gathered(0), gathered(1)
        square = hidden * hidden
        tanh = jnp.tanh(SCALE * (hidden + CUBIC * square * hidden))
        half_up = 0.5 * (1.0 + tanh)
        act = (hidden * half_up).astype(jnp.bfloat16)
        slope = half_up + (0.5 * hidden) * (1.0 - tanh * tanh) * (SCALE + (3.0 * CUBIC * SCALE) * square)
        d_hidden = (d_act * slope).astype(jnp.bfloat16)
        for side, right in enumerate((d_hidden, act)):
            left = picked_rows(table, buffers, side, base + step * LANES + lane, slots)
            total = lax.dot_general(left, right, (((0,), (0,)), ((), ())), preferred_element_type=jnp.float32)
            total = total.astype(jnp.bfloat16)
            own_ref[side, :, at] = total[:kept]
            away_ref[side, :, at] = total[kept:]


def grad(table, units, buffers, keeps, gots, kept, part, parts):
    width = max(keep.shape[2] for keep in keeps)
    wide = LANES * BLK
    steps = width // wide // parts

    def spec(array):
        first = part * steps if array.shape[2] == width else 0
        return pl.BlockSpec((2, array.shape[1], wide), lambda g, t: (0, 0, first + g))

    out = pl.BlockSpec((2, kept, wide), lambda g, t: (0, 0, g))
    return pl.pallas_call(
        functools.partial(
            grad_kernel, units, len(buffers), len(keeps), len(gots), 2 * kept // BLK, part * steps * LANES
        ),
        grid_spec=pltpu.PrefetchScalarGridSpec(
            num_scalar_prefetch=1,
            grid=(steps,),
            in_specs=[fixed(b) for b in buffers] + [spec(v) for v in (*keeps, *gots)],
            out_specs=[out, out],
        ),
        out_shape=[jax.ShapeDtypeStruct((2, kept, width // parts), jnp.bfloat16)] * 2,
        compiler_params=pltpu.CompilerParams(vmem_limit_bytes=GRAD_VMEM),
        cost_estimate=COST,
        name="grad",
    )(table, *buffers, *keeps, *gots)


def total_kernel(own_ref, got_ref, *refs):
    for side, ref in enumerate(refs[-2:]):
        ref[...] = (own_ref[side].astype(jnp.float32) + got_ref[side].astype(jnp.float32)).astype(ref.dtype)


def total(own, got, before, part, parts):
    kept, width = own.shape[1:]
    wide = TOTAL_LANES * BLK
    steps = width // wide
    source = pl.BlockSpec((2, kept, wide), lambda g: (0, 0, g))
    out = pl.BlockSpec((kept, wide), lambda g: (0, part * steps + g))
    return pl.pallas_call(
        total_kernel,
        grid=(steps,),
        in_specs=[source, source] + [pl.BlockSpec(memory_space=pl.ANY)] * len(before),
        out_specs=[out, out],
        out_shape=[jax.ShapeDtypeStruct((kept, width * parts), jnp.bfloat16)] * 2,
        input_output_aliases={2: 0, 3: 1} if before else {},
        compiler_params=pltpu.CompilerParams(vmem_limit_bytes=TOTAL_VMEM),
        cost_estimate=COST,
        name="total",
    )(own, got, *before)


def fast(inputs, cotangent, w_in, w_out, keep_in, keep_out):
    kept, width = w_in.shape
    here = width // BLK
    mine = kept // BLK
    row = lax.axis_index("row")
    col = lax.axis_index("col")

    def swap_x(v):
        return lax.ppermute(v, "row", [(r, r ^ 2) for r in range(ROWS)])

    def swap_core(v):
        return lax.ppermute(v, "row", [(r, r ^ 1) for r in range(ROWS)])

    def swap_y(v):
        return lax.ppermute(v, "col", [(c, c ^ 1) for c in range(COLS)])

    def near(v):
        return lax.ppermute(v, "col", [(c, c ^ 2) for c in range(COLS)])

    def far(v):
        return lax.ppermute(v, "col", [(c, c ^ 4) for c in range(COLS)])

    gate = lax.optimization_barrier

    a0 = jnp.stack((inputs, cotangent), 0)
    b0, ya0, a1 = swap_x(a0), swap_y(a0), near(a0)
    s_in, s_out = swap_core(w_in), swap_core(w_out)
    pieces = []
    for keep in (keep_in, keep_out):
        rows = lax.dynamic_slice_in_dim(keep, col * here, here, 0)
        pieces += [lax.dynamic_slice_in_dim(rows, r * mine, mine, 1) for r in (row, row ^ 1)]
    table = jnp.concatenate(pieces, axis=1).reshape(-1)
    held = [pltpu.with_memory_space_constraint(w, pltpu.HBM) for w in (w_in, w_out)]
    weights = pack(*held, s_in, s_out)
    table, weights, b0, ya0 = gate((table, weights, b0, ya0))
    yb0, b1, a2 = swap_y(b0), near(b0), far(a0)
    keep0, send0 = partial(table, (a0, ya0), weights)
    table, send0 = gate((table, send0))
    got0 = swap_x(send0)
    table, a1 = gate((table, a1))
    ya1 = swap_y(a1)
    table = tick(table)
    table, a2 = gate((table, a2))
    a3 = near(a2)
    table = tick(table)
    table, yb0, b0 = gate((table, yb0, b0))
    keep1, send1 = partial(table, (b0, yb0), weights)
    table, send1 = gate((table, send1))
    got1 = swap_x(send1)
    table, b1 = gate((table, b1))
    yb1 = swap_y(b1)
    table, got0, b0 = gate((table, got0, b0))
    b2 = far(b0)
    table, ya1, a1 = gate((table, ya1, a1))
    keep2, send2 = partial(table, (a1, ya1), weights)
    table, send2 = gate((table, send2))
    got2 = swap_x(send2)
    table, got1, a2 = gate((table, got1, a2))
    ya2 = swap_y(a2)
    table, yb1, b1 = gate((table, yb1, b1))
    keep3, send3 = partial(table, (b1, yb1), weights)
    table, send3 = gate((table, send3))
    got3 = swap_x(send3)
    table, a3 = gate((table, a3))
    ya3 = swap_y(a3)
    table, b2 = gate((table, b2))
    yb2, b3 = swap_y(b2), near(b2)
    table = tick(table)
    table, ya2, got2 = gate((table, ya2, got2))
    keep4, send4 = partial(table, (a2, ya2), weights)
    table, send4 = gate((table, send4))
    got4 = swap_x(send4)
    table, ya3, got3 = gate((table, ya3, got3))
    keep5, send5 = partial(table, (a3, ya3), weights)
    table, send5 = gate((table, send5))
    got5 = swap_x(send5)
    table, b3 = gate((table, b3))
    yb3 = swap_y(b3)
    table, yb2, got4 = gate((table, yb2, got4))
    keep6, send6 = partial(table, (b2, yb2), weights)
    table, send6 = gate((table, send6))
    got6 = swap_x(send6)
    table, yb3, b3 = gate((table, yb3, b3))
    keep7, got7 = [], []
    for part in range(PARTS):
        keep, send = partial(table, (b3, yb3), weights, part, PARTS)
        table, send = gate((table, send))
        if part == 0:
            table, got5 = gate((table, got5))
        keep7.append(keep)
        got7.append(swap_x(send))
    table, got6, got7[0] = gate((table, got6, got7[0]))

    buffers = (a0, ya0, b0, yb0, a1, ya1, b1, yb1, a2, ya2, a3, ya3, b2, yb2, b3, yb3)
    units = ((0, 0, 1, 0), (1, 0, 0, 0), (2, 0, 3, 0), (3, 0, 2, 0), (4, 0, 6, 0), (5, 0, 7, 0), (6, 0, 4, 0), (7, 0, 5, 0))
    keeps = (keep0, keep1, keep2, keep3, keep4, keep5, keep6)
    gots = (got0, got1, got2, got3, got4, got5, got6)
    outs, waiting = (), None
    for part in range(PARTS):
        own, away = grad(table, units, buffers, (*keeps, keep7[part]), (*gots, got7[part]), kept, part, PARTS)
        if part < PARTS - 1:
            table, own, away, got7[part + 1] = gate((table, own, away, got7[part + 1]))
        back = swap_core(away)
        if waiting is not None:
            outs = total(*waiting, outs, part - 1, PARTS)
        waiting = (own, back)
    return tuple(total(*waiting, tuple(outs), PARTS - 1, PARTS))


def solution(mesh):
    def per_device(inputs, cotangent, w_in, w_out, keep_in, keep_out):
        kept, width = w_in.shape
        fits = kept % BLK == 0 and inputs.shape[0] % 16 == 0
        fits = fits and all(width % (PARTS * lanes * BLK) == 0 for lanes in (LANES, PACK_LANES, TOTAL_LANES))
        chosen = fast if fits and mesh.shape["row"] == ROWS and mesh.shape["col"] == COLS else general
        return chosen(inputs, cotangent, w_in, w_out, keep_in, keep_out)

    in_specs = (
        P(("row", "col"), None),
        P(("row", "col"), None),
        P("row", "col"),
        P("row", "col"),
        P(),
        P(),
    )
    out_specs = (P("row", "col"), P("row", "col"))
    return jax.shard_map(
        per_device, mesh=mesh, in_specs=in_specs, out_specs=out_specs, check_vma=False
    )
```

```python
import functools

import jax
import jax.numpy as jnp
from jax import lax
from jax.experimental import pallas as pl
from jax.experimental.pallas import tpu as pltpu
from jax.sharding import PartitionSpec as P

D = 6144
BLK = 128
KEEP = 12
ROWS = 4
COLS = 8
LANES = 4
SCALE = 0.7978845608028654
CUBIC = 0.044715
PARTIAL_VMEM = 8 * 1024 * 1024
GRAD_VMEM = 16 * 1024 * 1024
TOTAL_VMEM = 8 * 1024 * 1024
PACK_ROWS = 64
TICK_VMEM = 1024 * 1024
PACK_VMEM = 12 * 1024 * 1024
PARTS = ((0, 2), (2, 2), (4, 2))
EARLY_VMEM = 8 * 1024 * 1024
COST = pl.CostEstimate(flops=0, bytes_accessed=0, transcendentals=0)


def gelu_tanh(values):
    return jax.nn.gelu(values, approximate=True)


def pick_one(matrix, chosen):
    return jnp.take(matrix, chosen, axis=1)


def general(inputs, cotangent, w_in, w_out, keep_in, keep_out):
    width = w_in.shape[1]
    blocks_here = width // BLK
    kept_rows = w_in.shape[0]
    column = lax.axis_index("col")
    own_in = lax.dynamic_slice_in_dim(keep_in, column * blocks_here, blocks_here, 0)
    own_out = lax.dynamic_slice_in_dim(keep_out, column * blocks_here, blocks_here, 0)
    tables = jnp.stack((own_in, own_out), 0)
    stacked = jnp.stack((inputs, cotangent), 0)
    whole = lax.all_gather(stacked, "col", axis=1, tiled=True)
    tokens_here = whole.shape[1]
    blocks = whole.reshape(2, tokens_here, D // BLK, BLK)
    picked = jax.vmap(pick_one)(blocks, tables).reshape(2, tokens_here, blocks_here, KEEP * BLK)
    weights = jnp.stack((w_in, w_out), 1)
    full = lax.all_gather(weights, "row", axis=0, tiled=True)
    panel = full.reshape(KEEP * BLK, 2, blocks_here, BLK)
    mixed = jnp.einsum("ptck,kpcq->ptcq", picked, panel, preferred_element_type=jnp.float32)
    hidden = mixed[0].reshape(tokens_here, width)
    d_act = mixed[1].reshape(tokens_here, width)
    act, pullback = jax.vjp(gelu_tanh, hidden)
    d_hidden = pullback(d_act)[0].astype(jnp.bfloat16)
    act = act.astype(jnp.bfloat16)
    paired = jnp.stack((d_hidden, act), 0).reshape(2, tokens_here, blocks_here, BLK)
    term = jnp.einsum("ptck,ptcq->kpcq", picked, paired, preferred_element_type=jnp.float32)
    summed = (
        lax.psum_scatter(
            term.reshape(lax.axis_size("row") * kept_rows, 2 * width).astype(jnp.bfloat16),
            "row",
            scatter_dimension=0,
            tiled=True,
        )
        .astype(jnp.float32)
        .reshape(kept_rows, 2, width)
    )
    return (summed[:, 0].astype(jnp.bfloat16), summed[:, 1].astype(jnp.bfloat16))


def picked_rows(table, buffers, side, block, slots):
    columns = []
    for slot in range(slots):
        start = pl.multiple_of(table[(block * 2 + side) * slots + slot] * BLK, BLK)
        columns.append(jnp.concatenate([buf[side, :, pl.ds(start, BLK)] for buf in buffers], axis=0))
    return jnp.concatenate(columns, axis=1)


def fixed(array):
    return pl.BlockSpec(array.shape, lambda g, t: (0,) * array.ndim, pipeline_mode=pl.Buffered(1))


def pack_kernel(*refs):
    for index, ref in enumerate(refs[:-1]):
        refs[-1][index] = ref[...]


def pack(*weights):
    kept, width = weights[0].shape
    return pl.pallas_call(
        pack_kernel,
        grid=(kept // PACK_ROWS,),
        in_specs=[pl.BlockSpec((PACK_ROWS, width), lambda g: (g, 0))] * len(weights),
        out_specs=pl.BlockSpec((len(weights), PACK_ROWS, width), lambda g: (0, g, 0)),
        out_shape=jax.ShapeDtypeStruct((len(weights), kept, width), weights[0].dtype),
        compiler_params=pltpu.CompilerParams(vmem_limit_bytes=PACK_VMEM),
        cost_estimate=COST,
        name="pack",
    )(*weights)


def partial_kernel(n_buf, slots, base, table, *refs):
    buffers = refs[:n_buf]
    weights, keep_ref, send_ref = refs[n_buf:]
    step = pl.program_id(0)
    for lane in range(LANES):
        at = slice(lane * BLK, (lane + 1) * BLK)
        for side in range(2):
            left = picked_rows(table, buffers, side, base + step * LANES + lane, slots)
            right = jnp.concatenate((weights[side, :, at], weights[2 + side, :, at]), axis=0)
            total = jnp.dot(left, right, preferred_element_type=jnp.float32)
            keep_ref[side, :, at] = total
            send_ref[side, :, at] = total.astype(jnp.bfloat16)


def partial(table, buffers, weights, first=0, steps=None):
    tokens = sum(b.shape[1] for b in buffers)
    kept, width = weights.shape[1:]
    wide = LANES * BLK
    steps = width // wide if steps is None else steps
    weight = pl.BlockSpec((4, kept, wide), lambda g, t: (0, 0, first + g))
    out = pl.BlockSpec((2, tokens, wide), lambda g, t: (0, 0, g))
    return pl.pallas_call(
        functools.partial(partial_kernel, len(buffers), 2 * kept // BLK, first * LANES),
        grid_spec=pltpu.PrefetchScalarGridSpec(
            num_scalar_prefetch=1,
            grid=(steps,),
            in_specs=[fixed(b) for b in buffers] + [weight],
            out_specs=[out, out],
        ),
        out_shape=[
            jax.ShapeDtypeStruct((2, tokens, steps * wide), dtype) for dtype in (jnp.float32, jnp.bfloat16)
        ],
        compiler_params=pltpu.CompilerParams(vmem_limit_bytes=PARTIAL_VMEM),
        cost_estimate=COST,
        name="partial",
    )(table, *buffers, weights)


def tick_kernel(table_ref, out_ref):
    pass


def tick(table):
    anywhere = pl.BlockSpec(memory_space=pl.ANY)
    return pl.pallas_call(
        tick_kernel,
        in_specs=[anywhere],
        out_specs=anywhere,
        out_shape=jax.ShapeDtypeStruct(table.shape, table.dtype),
        input_output_aliases={0: 0},
        compiler_params=pltpu.CompilerParams(vmem_limit_bytes=TICK_VMEM),
        cost_estimate=COST,
        name="tick",
    )(table)


def activations(keeps, gots, at):
    def summed(side):
        mine = jnp.concatenate([ref[side, :, at] for ref in keeps], axis=0)
        return mine + jnp.concatenate([ref[side, :, at] for ref in gots], axis=0).astype(jnp.float32)

    hidden, d_act = summed(0), summed(1)
    square = hidden * hidden
    tanh = jnp.tanh(SCALE * (hidden + CUBIC * square * hidden))
    half_up = 0.5 * (1.0 + tanh)
    slope = half_up + (0.5 * hidden) * (1.0 - tanh * tanh) * (SCALE + (3.0 * CUBIC * SCALE) * square)
    return (d_act * slope).astype(jnp.bfloat16), (hidden * half_up).astype(jnp.bfloat16)


def early_kernel(*refs):
    n = len(refs) // 2
    for lane in range(LANES):
        at = slice(lane * BLK, (lane + 1) * BLK)
        for side, value in enumerate(activations(refs[:n], refs[n : 2 * n], at)):
            refs[2 * n][side, :, at] = value


def early(keeps, gots):
    tokens = sum(v.shape[1] for v in keeps)
    width = keeps[0].shape[2]
    wide = LANES * BLK
    return pl.pallas_call(
        early_kernel,
        grid=(width // wide,),
        in_specs=[pl.BlockSpec((2, v.shape[1], wide), lambda g: (0, 0, g)) for v in (*keeps, *gots)],
        out_specs=pl.BlockSpec((2, tokens, wide), lambda g: (0, 0, g)),
        out_shape=jax.ShapeDtypeStruct((2, tokens, width), jnp.bfloat16),
        compiler_params=pltpu.CompilerParams(vmem_limit_bytes=EARLY_VMEM),
        cost_estimate=COST,
        name="early",
    )(*keeps, *gots)


def grad_kernel(n_buf, n_late, slots, base, table, *refs):
    buffers, done = refs[:n_buf], refs[n_buf]
    keeps = refs[n_buf + 1 : n_buf + 1 + n_late]
    gots = refs[n_buf + 1 + n_late : n_buf + 1 + 2 * n_late]
    own_ref, away_ref = refs[n_buf + 1 + 2 * n_late :]
    step = pl.program_id(0)
    kept = slots * BLK // 2
    for lane in range(LANES):
        at = slice(lane * BLK, (lane + 1) * BLK)
        for side, late in enumerate(activations(keeps, gots, at)):
            right = jnp.concatenate((done[side, :, at], late), axis=0)
            left = picked_rows(table, buffers, side, base + step * LANES + lane, slots)
            total = lax.dot_general(left, right, (((0,), (0,)), ((), ())), preferred_element_type=jnp.float32)
            total = total.astype(jnp.bfloat16)
            own_ref[side, :, at] = total[:kept]
            away_ref[side, :, at] = total[kept:]


def grad(table, buffers, done, keeps, gots, kept, first, steps):
    width = done.shape[2]
    wide = LANES * BLK

    def spec(array):
        start = first if array.shape[2] == width else 0
        return pl.BlockSpec((2, array.shape[1], wide), lambda g, t: (0, 0, start + g))

    out = pl.BlockSpec((2, kept, wide), lambda g, t: (0, 0, g))
    return pl.pallas_call(
        functools.partial(grad_kernel, len(buffers), len(keeps), 2 * kept // BLK, first * LANES),
        grid_spec=pltpu.PrefetchScalarGridSpec(
            num_scalar_prefetch=1,
            grid=(steps,),
            in_specs=[fixed(b) for b in buffers] + [spec(v) for v in (done, *keeps, *gots)],
            out_specs=[out, out],
        ),
        out_shape=[jax.ShapeDtypeStruct((2, kept, steps * wide), jnp.bfloat16)] * 2,
        compiler_params=pltpu.CompilerParams(vmem_limit_bytes=GRAD_VMEM),
        cost_estimate=COST,
        name="grad",
    )(table, *buffers, done, *keeps, *gots)


def total_kernel(own_ref, got_ref, *refs):
    for side, ref in enumerate(refs[-2:]):
        ref[...] = (own_ref[side].astype(jnp.float32) + got_ref[side].astype(jnp.float32)).astype(ref.dtype)


def total(own, got, before, first, width):
    kept, here = own.shape[1:]
    wide = LANES * BLK
    source = pl.BlockSpec((2, kept, wide), lambda g: (0, 0, g))
    out = pl.BlockSpec((kept, wide), lambda g: (0, first + g))
    return pl.pallas_call(
        total_kernel,
        grid=(here // wide,),
        in_specs=[source, source] + [pl.BlockSpec(memory_space=pl.ANY)] * len(before),
        out_specs=[out, out],
        out_shape=[jax.ShapeDtypeStruct((kept, width), jnp.bfloat16)] * 2,
        input_output_aliases={2: 0, 3: 1} if before else {},
        compiler_params=pltpu.CompilerParams(vmem_limit_bytes=TOTAL_VMEM),
        cost_estimate=COST,
        name="total",
    )(own, got, *before)


def fast(inputs, cotangent, w_in, w_out, keep_in, keep_out):
    kept, width = w_in.shape
    here = width // BLK
    mine = kept // BLK
    row = lax.axis_index("row")
    col = lax.axis_index("col")

    def swap_x(v):
        return lax.ppermute(v, "row", [(r, r ^ 2) for r in range(ROWS)])

    def swap_core(v):
        return lax.ppermute(v, "row", [(r, r ^ 1) for r in range(ROWS)])

    def swap_y(v):
        return lax.ppermute(v, "col", [(c, c ^ 1) for c in range(COLS)])

    def near(v):
        return lax.ppermute(v, "col", [(c, c ^ 2) for c in range(COLS)])

    def far(v):
        return lax.ppermute(v, "col", [(c, c ^ 4) for c in range(COLS)])

    gate = lax.optimization_barrier

    a0 = jnp.stack((inputs, cotangent), 0)
    b0, ya0, a1 = swap_x(a0), swap_y(a0), near(a0)
    s_in, s_out = swap_core(w_in), swap_core(w_out)
    pieces = []
    for keep in (keep_in, keep_out):
        rows = lax.dynamic_slice_in_dim(keep, col * here, here, 0)
        pieces += [lax.dynamic_slice_in_dim(rows, r * mine, mine, 1) for r in (row, row ^ 1)]
    table = jnp.concatenate(pieces, axis=1).reshape(-1)
    held = [pltpu.with_memory_space_constraint(w, pltpu.HBM) for w in (w_in, w_out)]
    weights = pack(*held, s_in, s_out)
    table, weights, b0, ya0 = gate((table, weights, b0, ya0))
    yb0, b1, a2 = swap_y(b0), near(b0), far(a0)
    keep0, send0 = partial(table, (a0, ya0), weights)
    table, send0 = gate((table, send0))
    got0 = swap_x(send0)
    table, a1 = gate((table, a1))
    ya1 = swap_y(a1)
    table = tick(table)
    table, a2 = gate((table, a2))
    a3 = near(a2)
    table = tick(table)
    table, yb0, b0 = gate((table, yb0, b0))
    keep1, send1 = partial(table, (b0, yb0), weights)
    table, send1 = gate((table, send1))
    got1 = swap_x(send1)
    table, b1 = gate((table, b1))
    yb1 = swap_y(b1)
    table, got0, b0 = gate((table, got0, b0))
    b2 = far(b0)
    table, ya1, a1 = gate((table, ya1, a1))
    keep2, send2 = partial(table, (a1, ya1), weights)
    table, send2 = gate((table, send2))
    got2 = swap_x(send2)
    table, got1, a2 = gate((table, got1, a2))
    ya2 = swap_y(a2)
    table, yb1, b1 = gate((table, yb1, b1))
    keep3, send3 = partial(table, (b1, yb1), weights)
    table, send3 = gate((table, send3))
    got3 = swap_x(send3)
    table, a3 = gate((table, a3))
    ya3 = swap_y(a3)
    table, b2 = gate((table, b2))
    yb2, b3 = swap_y(b2), near(b2)
    table = tick(table)
    table, ya2, got2 = gate((table, ya2, got2))
    keep4, send4 = partial(table, (a2, ya2), weights)
    table, send4 = gate((table, send4))
    got4 = swap_x(send4)
    table, ya3, got3 = gate((table, ya3, got3))
    keep5, send5 = partial(table, (a3, ya3), weights)
    table, send5 = gate((table, send5))
    got5 = swap_x(send5)
    table, b3 = gate((table, b3))
    yb3 = swap_y(b3)
    table, yb2, got4 = gate((table, yb2, got4))
    keep6, send6 = partial(table, (b2, yb2), weights)
    table, send6 = gate((table, send6))
    got6 = swap_x(send6)
    done = early((keep0, keep1, keep2, keep3, keep6), (got1, got0, got3, got2, got4))
    table, done = gate((table, done))
    table, yb3, b3 = gate((table, yb3, b3))
    keep7, got7 = [], []
    for part, (first, steps) in enumerate(PARTS):
        keep, send = partial(table, (b3, yb3), weights, first, steps)
        table, send = gate((table, send))
        if part == 0:
            table, got5 = gate((table, got5))
        keep7.append(keep)
        got7.append(swap_x(send))
    buffers = (a0, ya0, b0, yb0, a1, ya1, b1, yb1, b2, yb2, a2, ya2, a3, ya3, b3, yb3)
    table, got7[0] = gate((table, got7[0]))
    table, got6 = gate((table, got6))
    outs = ()
    for part, (first, steps) in enumerate(PARTS):
        keeps, gots = (keep4, keep5, keep7[part]), (got6, got7[part], got5)
        own, away = grad(table, buffers, done, keeps, gots, kept, first, steps)
        if part < len(PARTS) - 1:
            table, own, away, got7[part + 1] = gate((table, own, away, got7[part + 1]))
        back = swap_core(away)
        if part > 0:
            outs = total(*before, outs, PARTS[part - 1][0], width)
        before = [own, back]
    return tuple(total(*before, outs, PARTS[-1][0], width))


def solution(mesh):
    def per_device(inputs, cotangent, w_in, w_out, keep_in, keep_out):
        kept, width = w_in.shape
        fits = kept % BLK == 0 and inputs.shape[0] % 16 == 0
        fits = fits and kept % PACK_ROWS == 0 and width == sum(steps for _, steps in PARTS) * LANES * BLK
        chosen = fast if fits and mesh.shape["row"] == ROWS and mesh.shape["col"] == COLS else general
        return chosen(inputs, cotangent, w_in, w_out, keep_in, keep_out)

    in_specs = (
        P(("row", "col"), None),
        P(("row", "col"), None),
        P("row", "col"),
        P("row", "col"),
        P(),
        P(),
    )
    out_specs = (P("row", "col"), P("row", "col"))
    return jax.shard_map(
        per_device, mesh=mesh, in_specs=in_specs, out_specs=out_specs, check_vma=False
    )
```

```python
import functools

import jax
import jax.numpy as jnp
from jax import lax
from jax.experimental import pallas as pl
from jax.experimental.pallas import tpu as pltpu
from jax.sharding import PartitionSpec as P

D = 6144
BLK = 128
KEEP = 12
ROWS = 4
COLS = 8
LANES = 4
GRAD_LANES = 8
SCALE = 0.7978845608028654
CUBIC = 0.044715
PARTIAL_VMEM = 8 * 1024 * 1024
GRAD_VMEM = 20 * 1024 * 1024
TOTAL_VMEM = 14 * 1024 * 1024
TICK_VMEM = 1024 * 1024
PACK_VMEM = 1024 * 1024
PARTS = ((0, 2), (2, 2), (4, 2))
EARLY_VMEM = 8 * 1024 * 1024
COST = pl.CostEstimate(flops=0, bytes_accessed=0, transcendentals=0)


def gelu_tanh(values):
    return jax.nn.gelu(values, approximate=True)


def pick_one(matrix, chosen):
    return jnp.take(matrix, chosen, axis=1)


def general(inputs, cotangent, w_in, w_out, keep_in, keep_out):
    width = w_in.shape[1]
    blocks_here = width // BLK
    kept_rows = w_in.shape[0]
    column = lax.axis_index("col")
    own_in = lax.dynamic_slice_in_dim(keep_in, column * blocks_here, blocks_here, 0)
    own_out = lax.dynamic_slice_in_dim(keep_out, column * blocks_here, blocks_here, 0)
    tables = jnp.stack((own_in, own_out), 0)
    stacked = jnp.stack((inputs, cotangent), 0)
    whole = lax.all_gather(stacked, "col", axis=1, tiled=True)
    tokens_here = whole.shape[1]
    blocks = whole.reshape(2, tokens_here, D // BLK, BLK)
    picked = jax.vmap(pick_one)(blocks, tables).reshape(2, tokens_here, blocks_here, KEEP * BLK)
    weights = jnp.stack((w_in, w_out), 1)
    full = lax.all_gather(weights, "row", axis=0, tiled=True)
    panel = full.reshape(KEEP * BLK, 2, blocks_here, BLK)
    mixed = jnp.einsum("ptck,kpcq->ptcq", picked, panel, preferred_element_type=jnp.float32)
    hidden = mixed[0].reshape(tokens_here, width)
    d_act = mixed[1].reshape(tokens_here, width)
    act, pullback = jax.vjp(gelu_tanh, hidden)
    d_hidden = pullback(d_act)[0].astype(jnp.bfloat16)
    act = act.astype(jnp.bfloat16)
    paired = jnp.stack((d_hidden, act), 0).reshape(2, tokens_here, blocks_here, BLK)
    term = jnp.einsum("ptck,ptcq->kpcq", picked, paired, preferred_element_type=jnp.float32)
    summed = (
        lax.psum_scatter(
            term.reshape(lax.axis_size("row") * kept_rows, 2 * width).astype(jnp.bfloat16),
            "row",
            scatter_dimension=0,
            tiled=True,
        )
        .astype(jnp.float32)
        .reshape(kept_rows, 2, width)
    )
    return (summed[:, 0].astype(jnp.bfloat16), summed[:, 1].astype(jnp.bfloat16))


def picked_rows(table, buffers, side, block, slots):
    columns = []
    for slot in range(slots):
        start = pl.multiple_of(table[(block * 2 + side) * slots + slot] * BLK, BLK)
        columns.append(jnp.concatenate([buf[side, :, pl.ds(start, BLK)] for buf in buffers], axis=0))
    return jnp.concatenate(columns, axis=1)


def fixed(array):
    return pl.BlockSpec(array.shape, lambda g, t: (0,) * array.ndim, pipeline_mode=pl.Buffered(1))


def pack_kernel(*refs):
    sources, packed, sems = refs[:-2], refs[-2], refs[-1]
    copies = [pltpu.make_async_copy(ref, packed.at[i], sems.at[i]) for i, ref in enumerate(sources)]
    for copy in copies:
        copy.start()
    for copy in copies:
        copy.wait()


def pack(*weights):
    kept, width = weights[0].shape
    anywhere = pl.BlockSpec(memory_space=pl.ANY)
    return pl.pallas_call(
        pack_kernel,
        in_specs=[anywhere] * len(weights),
        out_specs=anywhere,
        out_shape=jax.ShapeDtypeStruct((len(weights), kept, width), weights[0].dtype),
        scratch_shapes=[pltpu.SemaphoreType.DMA((len(weights),))],
        compiler_params=pltpu.CompilerParams(vmem_limit_bytes=PACK_VMEM),
        cost_estimate=COST,
        name="pack",
    )(*weights)


def partial_kernel(n_buf, slots, base, table, *refs):
    buffers = refs[:n_buf]
    weights, keep_ref, send_ref = refs[n_buf:]
    step = pl.program_id(0)
    for lane in range(LANES):
        at = slice(lane * BLK, (lane + 1) * BLK)
        for side in range(2):
            left = picked_rows(table, buffers, side, base + step * LANES + lane, slots)
            right = jnp.concatenate((weights[side, :, at], weights[2 + side, :, at]), axis=0)
            total = jnp.dot(left, right, preferred_element_type=jnp.float32)
            keep_ref[side, :, at] = total
            send_ref[side, :, at] = total.astype(jnp.bfloat16)


def partial(table, buffers, weights, first=0, steps=None):
    tokens = sum(b.shape[1] for b in buffers)
    kept, width = weights.shape[1:]
    wide = LANES * BLK
    steps = width // wide if steps is None else steps
    weight = pl.BlockSpec((4, kept, wide), lambda g, t: (0, 0, first + g))
    out = pl.BlockSpec((2, tokens, wide), lambda g, t: (0, 0, g))
    return pl.pallas_call(
        functools.partial(partial_kernel, len(buffers), 2 * kept // BLK, first * LANES),
        grid_spec=pltpu.PrefetchScalarGridSpec(
            num_scalar_prefetch=1,
            grid=(steps,),
            in_specs=[fixed(b) for b in buffers] + [weight],
            out_specs=[out, out],
        ),
        out_shape=[
            jax.ShapeDtypeStruct((2, tokens, steps * wide), dtype) for dtype in (jnp.float32, jnp.bfloat16)
        ],
        compiler_params=pltpu.CompilerParams(vmem_limit_bytes=PARTIAL_VMEM),
        cost_estimate=COST,
        name="partial",
    )(table, *buffers, weights)


def tick_kernel(table_ref, out_ref):
    pass


def tick(table):
    anywhere = pl.BlockSpec(memory_space=pl.ANY)
    return pl.pallas_call(
        tick_kernel,
        in_specs=[anywhere],
        out_specs=anywhere,
        out_shape=jax.ShapeDtypeStruct(table.shape, table.dtype),
        input_output_aliases={0: 0},
        compiler_params=pltpu.CompilerParams(vmem_limit_bytes=TICK_VMEM),
        cost_estimate=COST,
        name="tick",
    )(table)


def activations(keeps, gots, at):
    def summed(side):
        mine = jnp.concatenate([ref[side, :, at] for ref in keeps], axis=0)
        return mine + jnp.concatenate([ref[side, :, at] for ref in gots], axis=0).astype(jnp.float32)

    hidden, d_act = summed(0), summed(1)
    square = hidden * hidden
    tanh = jnp.tanh(SCALE * (hidden + CUBIC * square * hidden))
    half_up = 0.5 * (1.0 + tanh)
    slope = half_up + (0.5 * hidden) * (1.0 - tanh * tanh) * (SCALE + (3.0 * CUBIC * SCALE) * square)
    return (d_act * slope).astype(jnp.bfloat16), (hidden * half_up).astype(jnp.bfloat16)


def early_kernel(*refs):
    n = len(refs) // 2
    for lane in range(LANES):
        at = slice(lane * BLK, (lane + 1) * BLK)
        for side, value in enumerate(activations(refs[:n], refs[n : 2 * n], at)):
            refs[2 * n][side, :, at] = value


def early(keeps, gots):
    tokens = sum(v.shape[1] for v in keeps)
    width = keeps[0].shape[2]
    wide = LANES * BLK
    return pl.pallas_call(
        early_kernel,
        grid=(width // wide,),
        in_specs=[pl.BlockSpec((2, v.shape[1], wide), lambda g: (0, 0, g)) for v in (*keeps, *gots)],
        out_specs=pl.BlockSpec((2, tokens, wide), lambda g: (0, 0, g)),
        out_shape=jax.ShapeDtypeStruct((2, tokens, width), jnp.bfloat16),
        compiler_params=pltpu.CompilerParams(vmem_limit_bytes=EARLY_VMEM),
        cost_estimate=COST,
        name="early",
    )(*keeps, *gots)


def grad_kernel(n_buf, n_late, slots, base, table, *refs):
    buffers, done = refs[:n_buf], refs[n_buf]
    keeps = refs[n_buf + 1 : n_buf + 1 + n_late]
    gots = refs[n_buf + 1 + n_late : n_buf + 1 + 2 * n_late]
    own_ref, away_ref = refs[n_buf + 1 + 2 * n_late :]
    step = pl.program_id(0)
    kept = slots * BLK // 2
    for lane in range(GRAD_LANES):
        at = slice(lane * BLK, (lane + 1) * BLK)
        for side, late in enumerate(activations(keeps, gots, at)):
            right = jnp.concatenate((done[side, :, at], late), axis=0)
            left = picked_rows(table, buffers, side, base + step * GRAD_LANES + lane, slots)
            total = lax.dot_general(left, right, (((0,), (0,)), ((), ())), preferred_element_type=jnp.float32)
            total = total.astype(jnp.bfloat16)
            own_ref[side, :, at] = total[:kept]
            away_ref[side, :, at] = total[kept:]


def grad(table, buffers, done, keeps, gots, kept, first, steps):
    width = done.shape[2]
    wide = GRAD_LANES * BLK
    begin, steps = first * LANES // GRAD_LANES, steps * LANES // GRAD_LANES

    def spec(array):
        start = begin if array.shape[2] == width else 0
        return pl.BlockSpec((2, array.shape[1], wide), lambda g, t: (0, 0, start + g))

    out = pl.BlockSpec((2, kept, wide), lambda g, t: (0, 0, g))
    return pl.pallas_call(
        functools.partial(grad_kernel, len(buffers), len(keeps), 2 * kept // BLK, first * LANES),
        grid_spec=pltpu.PrefetchScalarGridSpec(
            num_scalar_prefetch=1,
            grid=(steps,),
            in_specs=[fixed(b) for b in buffers] + [spec(v) for v in (done, *keeps, *gots)],
            out_specs=[out, out],
        ),
        out_shape=[jax.ShapeDtypeStruct((2, kept, steps * wide), jnp.bfloat16)] * 2,
        compiler_params=pltpu.CompilerParams(vmem_limit_bytes=GRAD_VMEM),
        cost_estimate=COST,
        name="grad",
    )(table, *buffers, done, *keeps, *gots)


def total_kernel(own_ref, got_ref, *refs):
    for side, ref in enumerate(refs[-2:]):
        ref[...] = (own_ref[side].astype(jnp.float32) + got_ref[side].astype(jnp.float32)).astype(ref.dtype)


def total(own, got, before, first, width):
    kept, here = own.shape[1:]
    wide = GRAD_LANES * BLK
    begin = first * LANES // GRAD_LANES
    source = pl.BlockSpec((2, kept, wide), lambda g: (0, 0, g))
    out = pl.BlockSpec((kept, wide), lambda g: (0, begin + g))
    return pl.pallas_call(
        total_kernel,
        grid=(here // wide,),
        in_specs=[source, source] + [pl.BlockSpec(memory_space=pl.ANY)] * len(before),
        out_specs=[out, out],
        out_shape=[jax.ShapeDtypeStruct((kept, width), jnp.bfloat16)] * 2,
        input_output_aliases={2: 0, 3: 1} if before else {},
        compiler_params=pltpu.CompilerParams(vmem_limit_bytes=TOTAL_VMEM),
        cost_estimate=COST,
        name="total",
    )(own, got, *before)


def fast(inputs, cotangent, w_in, w_out, keep_in, keep_out):
    kept, width = w_in.shape
    here = width // BLK
    mine = kept // BLK
    row = lax.axis_index("row")
    col = lax.axis_index("col")

    def swap_x(v):
        return lax.ppermute(v, "row", [(r, r ^ 2) for r in range(ROWS)])

    def swap_core(v):
        return lax.ppermute(v, "row", [(r, r ^ 1) for r in range(ROWS)])

    def swap_y(v):
        return lax.ppermute(v, "col", [(c, c ^ 1) for c in range(COLS)])

    def near(v):
        return lax.ppermute(v, "col", [(c, c ^ 2) for c in range(COLS)])

    def far(v):
        return lax.ppermute(v, "col", [(c, c ^ 4) for c in range(COLS)])

    gate = lax.optimization_barrier

    a0 = jnp.stack((inputs, cotangent), 0)
    b0, ya0, a1 = swap_x(a0), swap_y(a0), near(a0)
    s_in, s_out = swap_core(w_in), swap_core(w_out)
    pieces = []
    for keep in (keep_in, keep_out):
        rows = lax.dynamic_slice_in_dim(keep, col * here, here, 0)
        pieces += [lax.dynamic_slice_in_dim(rows, r * mine, mine, 1) for r in (row, row ^ 1)]
    table = jnp.concatenate(pieces, axis=1).reshape(-1)
    held = [pltpu.with_memory_space_constraint(w, pltpu.HBM) for w in (w_in, w_out)]
    weights = pack(*held, s_in, s_out)
    table, weights, b0, ya0 = gate((table, weights, b0, ya0))
    yb0, b1, a2 = swap_y(b0), near(b0), far(a0)
    keep0, send0 = partial(table, (a0, ya0), weights)
    table, send0 = gate((table, send0))
    got0 = swap_x(send0)
    table, a1 = gate((table, a1))
    ya1 = swap_y(a1)
    table = tick(table)
    table, a2 = gate((table, a2))
    a3 = near(a2)
    table = tick(table)
    table, yb0, b0 = gate((table, yb0, b0))
    keep1, send1 = partial(table, (b0, yb0), weights)
    table, send1 = gate((table, send1))
    got1 = swap_x(send1)
    table, b1 = gate((table, b1))
    yb1 = swap_y(b1)
    table, got0, b0 = gate((table, got0, b0))
    b2 = far(b0)
    table, ya1, a1 = gate((table, ya1, a1))
    keep2, send2 = partial(table, (a1, ya1), weights)
    table, send2 = gate((table, send2))
    got2 = swap_x(send2)
    table, got1, a2 = gate((table, got1, a2))
    ya2 = swap_y(a2)
    table, yb1, b1 = gate((table, yb1, b1))
    keep3, send3 = partial(table, (b1, yb1), weights)
    table, send3 = gate((table, send3))
    got3 = swap_x(send3)
    table, a3 = gate((table, a3))
    ya3 = swap_y(a3)
    table, b2 = gate((table, b2))
    yb2, b3 = swap_y(b2), near(b2)
    table = tick(table)
    table, ya2, got2 = gate((table, ya2, got2))
    keep4, send4 = partial(table, (a2, ya2), weights)
    table, send4 = gate((table, send4))
    got4 = swap_x(send4)
    table, ya3, got3 = gate((table, ya3, got3))
    keep5, send5 = partial(table, (a3, ya3), weights)
    table, send5 = gate((table, send5))
    got5 = swap_x(send5)
    table, b3 = gate((table, b3))
    yb3 = swap_y(b3)
    table, yb2, got4 = gate((table, yb2, got4))
    keep6, send6 = partial(table, (b2, yb2), weights)
    table, send6 = gate((table, send6))
    got6 = swap_x(send6)
    done = early((keep0, keep1, keep2, keep3, keep6), (got1, got0, got3, got2, got4))
    table, done = gate((table, done))
    table, yb3, b3 = gate((table, yb3, b3))
    keep7, got7 = [], []
    for part, (first, steps) in enumerate(PARTS):
        keep, send = partial(table, (b3, yb3), weights, first, steps)
        table, send = gate((table, send))
        if part == 0:
            table, got5 = gate((table, got5))
        keep7.append(keep)
        got7.append(swap_x(send))
    buffers = (a0, ya0, b0, yb0, a1, ya1, b1, yb1, b2, yb2, a2, ya2, a3, ya3, b3, yb3)
    table, got7[0] = gate((table, got7[0]))
    table, got6 = gate((table, got6))
    outs = ()
    for part, (first, steps) in enumerate(PARTS):
        keeps, gots = (keep4, keep5, keep7[part]), (got6, got7[part], got5)
        own, away = grad(table, buffers, done, keeps, gots, kept, first, steps)
        if part < len(PARTS) - 1:
            table, own, away, got7[part + 1] = gate((table, own, away, got7[part + 1]))
        back = swap_core(away)
        if part > 0:
            outs = total(*before, outs, PARTS[part - 1][0], width)
        before = [own, back]
    return tuple(total(*before, outs, PARTS[-1][0], width))


def solution(mesh):
    def per_device(inputs, cotangent, w_in, w_out, keep_in, keep_out):
        kept, width = w_in.shape
        fits = kept % BLK == 0 and inputs.shape[0] % 16 == 0
        fits = fits and all(v * LANES % GRAD_LANES == 0 for part in PARTS for v in part)
        fits = fits and width == sum(steps for _, steps in PARTS) * LANES * BLK
        chosen = fast if fits and mesh.shape["row"] == ROWS and mesh.shape["col"] == COLS else general
        return chosen(inputs, cotangent, w_in, w_out, keep_in, keep_out)

    in_specs = (
        P(("row", "col"), None),
        P(("row", "col"), None),
        P("row", "col"),
        P("row", "col"),
        P(),
        P(),
    )
    out_specs = (P("row", "col"), P("row", "col"))
    return jax.shard_map(
        per_device, mesh=mesh, in_specs=in_specs, out_specs=out_specs, check_vma=False
    )
```

```python
import functools

import jax
import jax.numpy as jnp
from jax import lax
from jax.experimental import pallas as pl
from jax.experimental.pallas import tpu as pltpu
from jax.sharding import PartitionSpec as P

D = 6144
BLK = 128
KEEP = 12
ROWS = 4
COLS = 8
LANES = 4
FULL_LANES = 6
GRAD_LANES = 8
SCALE = 0.7978845608028654
CUBIC = 0.044715
PARTIAL_VMEM = 10 * 1024 * 1024
GRAD_VMEM = 20 * 1024 * 1024
TOTAL_VMEM = 14 * 1024 * 1024
TICK_VMEM = 1024 * 1024
PACK_VMEM = 1024 * 1024
PARTS = ((0, 2), (2, 2), (4, 2))
EARLY_VMEM = 8 * 1024 * 1024
COST = pl.CostEstimate(flops=0, bytes_accessed=0, transcendentals=0)


def gelu_tanh(values):
    return jax.nn.gelu(values, approximate=True)


def pick_one(matrix, chosen):
    return jnp.take(matrix, chosen, axis=1)


def general(inputs, cotangent, w_in, w_out, keep_in, keep_out):
    width = w_in.shape[1]
    blocks_here = width // BLK
    kept_rows = w_in.shape[0]
    column = lax.axis_index("col")
    own_in = lax.dynamic_slice_in_dim(keep_in, column * blocks_here, blocks_here, 0)
    own_out = lax.dynamic_slice_in_dim(keep_out, column * blocks_here, blocks_here, 0)
    tables = jnp.stack((own_in, own_out), 0)
    stacked = jnp.stack((inputs, cotangent), 0)
    whole = lax.all_gather(stacked, "col", axis=1, tiled=True)
    tokens_here = whole.shape[1]
    blocks = whole.reshape(2, tokens_here, D // BLK, BLK)
    picked = jax.vmap(pick_one)(blocks, tables).reshape(2, tokens_here, blocks_here, KEEP * BLK)
    weights = jnp.stack((w_in, w_out), 1)
    full = lax.all_gather(weights, "row", axis=0, tiled=True)
    panel = full.reshape(KEEP * BLK, 2, blocks_here, BLK)
    mixed = jnp.einsum("ptck,kpcq->ptcq", picked, panel, preferred_element_type=jnp.float32)
    hidden = mixed[0].reshape(tokens_here, width)
    d_act = mixed[1].reshape(tokens_here, width)
    act, pullback = jax.vjp(gelu_tanh, hidden)
    d_hidden = pullback(d_act)[0].astype(jnp.bfloat16)
    act = act.astype(jnp.bfloat16)
    paired = jnp.stack((d_hidden, act), 0).reshape(2, tokens_here, blocks_here, BLK)
    term = jnp.einsum("ptck,ptcq->kpcq", picked, paired, preferred_element_type=jnp.float32)
    summed = (
        lax.psum_scatter(
            term.reshape(lax.axis_size("row") * kept_rows, 2 * width).astype(jnp.bfloat16),
            "row",
            scatter_dimension=0,
            tiled=True,
        )
        .astype(jnp.float32)
        .reshape(kept_rows, 2, width)
    )
    return (summed[:, 0].astype(jnp.bfloat16), summed[:, 1].astype(jnp.bfloat16))


def picked_rows(table, buffers, side, block, slots):
    columns = []
    for slot in range(slots):
        start = pl.multiple_of(table[(block * 2 + side) * slots + slot] * BLK, BLK)
        columns.append(jnp.concatenate([buf[side, :, pl.ds(start, BLK)] for buf in buffers], axis=0))
    return jnp.concatenate(columns, axis=1)


def fixed(array):
    return pl.BlockSpec(array.shape, lambda g, t: (0,) * array.ndim, pipeline_mode=pl.Buffered(1))


def pack_kernel(*refs):
    sources, packed, sems = refs[:-2], refs[-2], refs[-1]
    copies = [pltpu.make_async_copy(ref, packed.at[i], sems.at[i]) for i, ref in enumerate(sources)]
    for copy in copies:
        copy.start()
    for copy in copies:
        copy.wait()


def pack(*weights):
    kept, width = weights[0].shape
    anywhere = pl.BlockSpec(memory_space=pl.ANY)
    return pl.pallas_call(
        pack_kernel,
        in_specs=[anywhere] * len(weights),
        out_specs=anywhere,
        out_shape=jax.ShapeDtypeStruct((len(weights), kept, width), weights[0].dtype),
        scratch_shapes=[pltpu.SemaphoreType.DMA((len(weights),))],
        compiler_params=pltpu.CompilerParams(vmem_limit_bytes=PACK_VMEM),
        cost_estimate=COST,
        name="pack",
    )(*weights)


def partial_kernel(n_buf, slots, base, lanes, table, *refs):
    buffers = refs[:n_buf]
    weights, keep_ref, send_ref = refs[n_buf:]
    step = pl.program_id(0)
    for lane in range(lanes):
        at = slice(lane * BLK, (lane + 1) * BLK)
        for side in range(2):
            left = picked_rows(table, buffers, side, base + step * lanes + lane, slots)
            right = jnp.concatenate((weights[side, :, at], weights[2 + side, :, at]), axis=0)
            total = jnp.dot(left, right, preferred_element_type=jnp.float32)
            keep_ref[side, :, at] = total
            send_ref[side, :, at] = total.astype(jnp.bfloat16)


def partial(table, buffers, weights, first=0, steps=None):
    tokens = sum(b.shape[1] for b in buffers)
    kept, width = weights.shape[1:]
    lanes = FULL_LANES if steps is None else LANES
    wide = lanes * BLK
    steps = width // wide if steps is None else steps
    weight = pl.BlockSpec((4, kept, wide), lambda g, t: (0, 0, first + g))
    out = pl.BlockSpec((2, tokens, wide), lambda g, t: (0, 0, g))
    return pl.pallas_call(
        functools.partial(partial_kernel, len(buffers), 2 * kept // BLK, first * lanes, lanes),
        grid_spec=pltpu.PrefetchScalarGridSpec(
            num_scalar_prefetch=1,
            grid=(steps,),
            in_specs=[fixed(b) for b in buffers] + [weight],
            out_specs=[out, out],
        ),
        out_shape=[
            jax.ShapeDtypeStruct((2, tokens, steps * wide), dtype) for dtype in (jnp.float32, jnp.bfloat16)
        ],
        compiler_params=pltpu.CompilerParams(vmem_limit_bytes=PARTIAL_VMEM),
        cost_estimate=COST,
        name="partial",
    )(table, *buffers, weights)


def tick_kernel(table_ref, out_ref):
    pass


def tick(table):
    anywhere = pl.BlockSpec(memory_space=pl.ANY)
    return pl.pallas_call(
        tick_kernel,
        in_specs=[anywhere],
        out_specs=anywhere,
        out_shape=jax.ShapeDtypeStruct(table.shape, table.dtype),
        input_output_aliases={0: 0},
        compiler_params=pltpu.CompilerParams(vmem_limit_bytes=TICK_VMEM),
        cost_estimate=COST,
        name="tick",
    )(table)


def activations(keeps, gots, at):
    def summed(side):
        mine = jnp.concatenate([ref[side, :, at] for ref in keeps], axis=0)
        return mine + jnp.concatenate([ref[side, :, at] for ref in gots], axis=0).astype(jnp.float32)

    hidden, d_act = summed(0), summed(1)
    square = hidden * hidden
    tanh = jnp.tanh(SCALE * (hidden + CUBIC * square * hidden))
    half_up = 0.5 * (1.0 + tanh)
    slope = half_up + (0.5 * hidden) * (1.0 - tanh * tanh) * (SCALE + (3.0 * CUBIC * SCALE) * square)
    return (d_act * slope).astype(jnp.bfloat16), (hidden * half_up).astype(jnp.bfloat16)


def early_kernel(*refs):
    n = len(refs) // 2
    for lane in range(LANES):
        at = slice(lane * BLK, (lane + 1) * BLK)
        for side, value in enumerate(activations(refs[:n], refs[n : 2 * n], at)):
            refs[2 * n][side, :, at] = value


def early(keeps, gots):
    tokens = sum(v.shape[1] for v in keeps)
    width = keeps[0].shape[2]
    wide = LANES * BLK
    return pl.pallas_call(
        early_kernel,
        grid=(width // wide,),
        in_specs=[pl.BlockSpec((2, v.shape[1], wide), lambda g: (0, 0, g)) for v in (*keeps, *gots)],
        out_specs=pl.BlockSpec((2, tokens, wide), lambda g: (0, 0, g)),
        out_shape=jax.ShapeDtypeStruct((2, tokens, width), jnp.bfloat16),
        compiler_params=pltpu.CompilerParams(vmem_limit_bytes=EARLY_VMEM),
        cost_estimate=COST,
        name="early",
    )(*keeps, *gots)


def grad_kernel(n_buf, n_late, slots, base, table, *refs):
    buffers, done = refs[:n_buf], refs[n_buf]
    keeps = refs[n_buf + 1 : n_buf + 1 + n_late]
    gots = refs[n_buf + 1 + n_late : n_buf + 1 + 2 * n_late]
    own_ref, away_ref = refs[n_buf + 1 + 2 * n_late :]
    step = pl.program_id(0)
    kept = slots * BLK // 2
    for lane in range(GRAD_LANES):
        at = slice(lane * BLK, (lane + 1) * BLK)
        for side, late in enumerate(activations(keeps, gots, at)):
            right = jnp.concatenate((done[side, :, at], late), axis=0)
            left = picked_rows(table, buffers, side, base + step * GRAD_LANES + lane, slots)
            total = lax.dot_general(left, right, (((0,), (0,)), ((), ())), preferred_element_type=jnp.float32)
            total = total.astype(jnp.bfloat16)
            own_ref[side, :, at] = total[:kept]
            away_ref[side, :, at] = total[kept:]


def grad(table, buffers, done, keeps, gots, kept, first, steps):
    width = done.shape[2]
    wide = GRAD_LANES * BLK
    begin, steps = first * LANES // GRAD_LANES, steps * LANES // GRAD_LANES

    def spec(array):
        start = begin if array.shape[2] == width else 0
        return pl.BlockSpec((2, array.shape[1], wide), lambda g, t: (0, 0, start + g))

    out = pl.BlockSpec((2, kept, wide), lambda g, t: (0, 0, g))
    return pl.pallas_call(
        functools.partial(grad_kernel, len(buffers), len(keeps), 2 * kept // BLK, first * LANES),
        grid_spec=pltpu.PrefetchScalarGridSpec(
            num_scalar_prefetch=1,
            grid=(steps,),
            in_specs=[fixed(b) for b in buffers] + [spec(v) for v in (done, *keeps, *gots)],
            out_specs=[out, out],
        ),
        out_shape=[jax.ShapeDtypeStruct((2, kept, steps * wide), jnp.bfloat16)] * 2,
        compiler_params=pltpu.CompilerParams(vmem_limit_bytes=GRAD_VMEM),
        cost_estimate=COST,
        name="grad",
    )(table, *buffers, done, *keeps, *gots)


def total_kernel(own_ref, got_ref, *refs):
    for side, ref in enumerate(refs[-2:]):
        ref[...] = (own_ref[side].astype(jnp.float32) + got_ref[side].astype(jnp.float32)).astype(ref.dtype)


def total(own, got, before, first, width):
    kept, here = own.shape[1:]
    wide = GRAD_LANES * BLK
    begin = first * LANES // GRAD_LANES
    source = pl.BlockSpec((2, kept, wide), lambda g: (0, 0, g))
    out = pl.BlockSpec((kept, wide), lambda g: (0, begin + g))
    return pl.pallas_call(
        total_kernel,
        grid=(here // wide,),
        in_specs=[source, source] + [pl.BlockSpec(memory_space=pl.ANY)] * len(before),
        out_specs=[out, out],
        out_shape=[jax.ShapeDtypeStruct((kept, width), jnp.bfloat16)] * 2,
        input_output_aliases={2: 0, 3: 1} if before else {},
        compiler_params=pltpu.CompilerParams(vmem_limit_bytes=TOTAL_VMEM),
        cost_estimate=COST,
        name="total",
    )(own, got, *before)


def fast(inputs, cotangent, w_in, w_out, keep_in, keep_out):
    kept, width = w_in.shape
    here = width // BLK
    mine = kept // BLK
    row = lax.axis_index("row")
    col = lax.axis_index("col")

    def swap_x(v):
        return lax.ppermute(v, "row", [(r, r ^ 2) for r in range(ROWS)])

    def swap_core(v):
        return lax.ppermute(v, "row", [(r, r ^ 1) for r in range(ROWS)])

    def swap_y(v):
        return lax.ppermute(v, "col", [(c, c ^ 1) for c in range(COLS)])

    def near(v):
        return lax.ppermute(v, "col", [(c, c ^ 2) for c in range(COLS)])

    def far(v):
        return lax.ppermute(v, "col", [(c, c ^ 4) for c in range(COLS)])

    gate = lax.optimization_barrier

    a0 = jnp.stack((inputs, cotangent), 0)
    b0, ya0, a1 = swap_x(a0), swap_y(a0), near(a0)
    s_in, s_out = swap_core(w_in), swap_core(w_out)
    pieces = []
    for keep in (keep_in, keep_out):
        rows = lax.dynamic_slice_in_dim(keep, col * here, here, 0)
        pieces += [lax.dynamic_slice_in_dim(rows, r * mine, mine, 1) for r in (row, row ^ 1)]
    table = jnp.concatenate(pieces, axis=1).reshape(-1)
    held = [pltpu.with_memory_space_constraint(w, pltpu.HBM) for w in (w_in, w_out)]
    weights = pack(*held, s_in, s_out)
    table, weights, b0, ya0 = gate((table, weights, b0, ya0))
    yb0, b1, a2 = swap_y(b0), near(b0), far(a0)
    keep0, send0 = partial(table, (a0, ya0), weights)
    table, send0 = gate((table, send0))
    got0 = swap_x(send0)
    table, a1 = gate((table, a1))
    ya1 = swap_y(a1)
    table = tick(table)
    table, a2 = gate((table, a2))
    a3 = near(a2)
    table = tick(table)
    table, yb0, b0 = gate((table, yb0, b0))
    keep1, send1 = partial(table, (b0, yb0), weights)
    table, send1 = gate((table, send1))
    got1 = swap_x(send1)
    table, b1 = gate((table, b1))
    yb1 = swap_y(b1)
    table, got0, b0 = gate((table, got0, b0))
    b2 = far(b0)
    table, ya1, a1 = gate((table, ya1, a1))
    keep2, send2 = partial(table, (a1, ya1), weights)
    table, send2 = gate((table, send2))
    got2 = swap_x(send2)
    table, got1, a2 = gate((table, got1, a2))
    ya2 = swap_y(a2)
    table, yb1, b1 = gate((table, yb1, b1))
    keep3, send3 = partial(table, (b1, yb1), weights)
    table, send3 = gate((table, send3))
    got3 = swap_x(send3)
    table, a3 = gate((table, a3))
    ya3 = swap_y(a3)
    table, b2 = gate((table, b2))
    yb2, b3 = swap_y(b2), near(b2)
    table = tick(table)
    table, ya2, got2 = gate((table, ya2, got2))
    keep4, send4 = partial(table, (a2, ya2), weights)
    table, send4 = gate((table, send4))
    got4 = swap_x(send4)
    table, ya3, got3 = gate((table, ya3, got3))
    keep5, send5 = partial(table, (a3, ya3), weights)
    table, send5 = gate((table, send5))
    got5 = swap_x(send5)
    table, b3 = gate((table, b3))
    yb3 = swap_y(b3)
    table, yb2, got4 = gate((table, yb2, got4))
    keep6, send6 = partial(table, (b2, yb2), weights)
    table, send6 = gate((table, send6))
    got6 = swap_x(send6)
    done = early((keep0, keep1, keep2, keep3, keep6), (got1, got0, got3, got2, got4))
    table, done = gate((table, done))
    table, yb3, b3 = gate((table, yb3, b3))
    keep7, got7 = [], []
    for part, (first, steps) in enumerate(PARTS):
        keep, send = partial(table, (b3, yb3), weights, first, steps)
        table, send = gate((table, send))
        if part == 0:
            table, got5 = gate((table, got5))
        keep7.append(keep)
        got7.append(swap_x(send))
    buffers = (a0, ya0, b0, yb0, a1, ya1, b1, yb1, b2, yb2, a2, ya2, a3, ya3, b3, yb3)
    table, got7[0] = gate((table, got7[0]))
    table, got6 = gate((table, got6))
    outs = ()
    for part, (first, steps) in enumerate(PARTS):
        keeps, gots = (keep4, keep5, keep7[part]), (got6, got7[part], got5)
        own, away = grad(table, buffers, done, keeps, gots, kept, first, steps)
        if part < len(PARTS) - 1:
            table, own, away, got7[part + 1] = gate((table, own, away, got7[part + 1]))
        back = swap_core(away)
        if part > 0:
            outs = total(*before, outs, PARTS[part - 1][0], width)
        before = [own, back]
    return tuple(total(*before, outs, PARTS[-1][0], width))


def solution(mesh):
    def per_device(inputs, cotangent, w_in, w_out, keep_in, keep_out):
        kept, width = w_in.shape
        fits = kept % BLK == 0 and inputs.shape[0] % 16 == 0
        fits = fits and all(v * LANES % GRAD_LANES == 0 for part in PARTS for v in part)
        fits = fits and width % (FULL_LANES * BLK) == 0
        fits = fits and width == sum(steps for _, steps in PARTS) * LANES * BLK
        chosen = fast if fits and mesh.shape["row"] == ROWS and mesh.shape["col"] == COLS else general
        return chosen(inputs, cotangent, w_in, w_out, keep_in, keep_out)

    in_specs = (
        P(("row", "col"), None),
        P(("row", "col"), None),
        P("row", "col"),
        P("row", "col"),
        P(),
        P(),
    )
    out_specs = (P("row", "col"), P("row", "col"))
    return jax.shard_map(
        per_device, mesh=mesh, in_specs=in_specs, out_specs=out_specs, check_vma=False
    )
```
